256 devices in a mesh: dom: 256 (over y, x, z, core).
Axes of the slice: x: 4, y: 4, z: 8, core: 2. Of those that a mesh axis runs over, the one named last changes fastest.
Arguments:
- features: bfloat16 [524288, 128], P('dom'), may hold values from -6 to 6
- w_self: bfloat16 [128, 256], replicated, may hold values from -0.5 to 0.5
- w_neigh: bfloat16 [128, 256], replicated, may hold values from -1.75 to 1.75
- cotangent: bfloat16 [524288, 256], P('dom'), may hold values from -6 to 6
- neighbours: int32 [524288, 10], P('dom'), may hold values from 0 to 3327, as said below
- send_rows: int32 [256, 5, 256], P('dom'), may hold values from 0 to 2047, as said below
- send_count: int32 [256, 5], P('dom'), may hold values from 64 to 256, as said below
Outputs:
- hidden: bfloat16 [524288, 256], P('dom')
- grad_features: float32 [524288, 128], P('dom')
- grad_self: float32 [128, 256], replicated
- grad_neigh: float32 [128, 256], replicated
The draws below stay inside these ranges and needn't reach their ends.
Inputs may be any that keep to these rules, and one draw needn't show every extreme that they name: `neighbours`: entries below 2048 name the partition's own rows; an entry 2048 + b * 256 + c names slot c of round b from partner p XOR 2^b, and c is below that partner's send_count for round b. `send_rows`: local row numbers, all different within one partition's round. Slots 0 to send_count - 1 of a round are live.
All inputs are finite; a program needn't handle non-finite values.
Results may differ from the reference program's by a relative error of at most 0.0059.
Values may be sent and summed in bfloat16 or wider, within the bound.
A program may use at most 64 MiB of HBM per device.

```python
import jax
import jax.numpy as jnp
from jax import lax

D_IN = 128
HID = 256
ROWS = 2048
FAN = 10
ROUNDS = 5
CAP = 256
NODES = 524288
N_DOM = 256


def shared_counts(key):
    count_key = jax.random.fold_in(key, 7)
    counts = jax.random.randint(count_key, (N_DOM, ROUNDS), CAP // 4, CAP + 1)
    fullest = jax.random.randint(jax.random.fold_in(count_key, 1), (ROUNDS,), 0, N_DOM)
    offset = jax.random.randint(jax.random.fold_in(count_key, 2), (ROUNDS,), 1, N_DOM)
    lowest = (fullest + offset) % N_DOM
    device = jnp.arange(N_DOM, dtype=jnp.int32)[:, None]
    counts = jnp.where(device == fullest[None, :], CAP, counts)
    counts = jnp.where(device == lowest[None, :], CAP // 4, counts)
    return (counts.astype(jnp.int32), fullest.astype(jnp.int32))


def draw_send_count(key, part):
    counts, fullest = shared_counts(key)
    return counts


def draw_send_rows(key, part):
    key = jax.random.fold_in(key, 11)
    keys = jax.random.split(key, N_DOM * ROUNDS)
    picks = jax.vmap(lambda single: jax.random.permutation(single, ROWS)[:CAP])(keys)
    return picks.reshape(N_DOM, ROUNDS, CAP).astype(jnp.int32)


def draw_neighbours(key, part):
    counts, fullest = shared_counts(key)
    key = jax.random.fold_in(key, 13)
    shape = (N_DOM, ROWS, FAN)
    source = jax.random.randint(jax.random.fold_in(key, 1), shape, 0, 2 * ROUNDS)
    local = jax.random.randint(jax.random.fold_in(key, 2), shape, 0, ROWS)
    raw = jax.random.randint(jax.random.fold_in(key, 3), shape, 0, 1 << 20)
    device = jnp.arange(N_DOM, dtype=jnp.int32)[:, None, None]
    round_pick = jnp.minimum(source, ROUNDS - 1)
    partner = jnp.bitwise_xor(device, jnp.left_shift(jnp.int32(1), round_pick))
    limit = counts[partner, round_pick]
    halo = ROWS + round_pick * CAP + raw % limit
    chosen = jnp.where(source < ROUNDS, halo, local)
    target = jnp.bitwise_xor(fullest[ROUNDS - 1], 1 << ROUNDS - 1)
    row_pick = jax.random.randint(jax.random.fold_in(key, 4), (), 0, ROWS)
    row_ids = jnp.arange(ROWS, dtype=jnp.int32)[None, :, None]
    fan_ids = jnp.arange(FAN, dtype=jnp.int32)[None, None, :]
    marked = (device == target) & (row_ids == row_pick)
    chosen = jnp.where(marked & (fan_ids == 0), ROWS + ROUNDS * CAP - 1, chosen)
    chosen = jnp.where(marked & (fan_ids == 1), 0, chosen)
    return chosen.reshape(N_DOM * ROWS, FAN).astype(jnp.int32)


def block_scale(key, extent, shards, low, top_value):
    gain = 1.0
    for axis_at, shards_of in shards:
        draws = jax.random.uniform(jax.random.fold_in(jax.random.fold_in(key, 6), axis_at), (shards_of,), jnp.float32, low / len(shards), top_value / len(shards))
        gain = gain * jnp.repeat(jnp.exp(draws), extent[axis_at] // shards_of).reshape((-1,) + (1,) * (len(extent) - 1 - axis_at))
    return gain


def noise(key, extent, scale, bound, shards=(), held_as=jnp.bfloat16):
    level = block_scale(key, extent, shards, -0.22, 0.18) if shards else 1.0
    array = jax.random.normal(key, extent, jnp.float32) * scale * level
    return jnp.minimum(jnp.maximum(array, -bound), bound).astype(held_as)


def setup_inputs(seed: int = 0) -> dict:
    arg_keys = jax.random.split(jax.random.key(seed), 8)
    return {
        "features": noise(arg_keys[0], (NODES, D_IN), 1.0, 6.0, ((0, 256),)),
        "w_self": noise(arg_keys[1], (D_IN, HID), D_IN ** -0.5, 0.5),
        "w_neigh": noise(arg_keys[2], (D_IN, HID), (D_IN // FAN) ** -0.5, 1.75),
        "cotangent": noise(arg_keys[3], (NODES, HID), 1.0, 6.0, ((0, 256),)),
        "neighbours": draw_neighbours(jax.random.fold_in(arg_keys[7], 71), 0),
        "send_rows": draw_send_rows(jax.random.fold_in(arg_keys[7], 71), 0),
        "send_count": draw_send_count(jax.random.fold_in(arg_keys[7], 71), 0),
    }


def silu_slope(pre):
    sig = jax.nn.sigmoid(pre)
    return sig * (1.0 + pre * (1.0 - sig))


def reference(features, w_self, w_neigh, cotangent, neighbours, send_rows, send_count):
    feat = features.reshape(N_DOM, ROWS, D_IN)
    slot = jnp.arange(CAP, dtype=jnp.int32)
    live = (slot[None, None, :] < send_count[:, :, None]).astype(jnp.float32)

    def pack(args):
        block, rows_sent, alive = args
        return block[rows_sent] * alive[:, :, None].astype(jnp.bfloat16)

    sent = lax.map(pack, (feat, send_rows, live))
    device = jnp.arange(N_DOM, dtype=jnp.int32)
    round_ids = jnp.arange(ROUNDS, dtype=jnp.int32)
    partner = jnp.bitwise_xor(device[:, None], jnp.left_shift(jnp.int32(1), round_ids)[None, :])
    received = sent[partner, round_ids[None, :]]
    nbr = neighbours.reshape(N_DOM, ROWS, FAN)
    cot = cotangent.reshape(N_DOM, ROWS, HID)
    contract = (((0,), (0,)), ((), ()))
    trans = (((1,), (1,)), ((), ()))

    def forward(args):
        block, recv, nb, ct = args
        table = jnp.concatenate([block, recv.reshape(ROUNDS * CAP, D_IN)], 0)
        mean_rows = (jnp.sum(table[nb].astype(jnp.float32), axis=1) / FAN).astype(jnp.bfloat16)
        pre = jnp.dot(block, w_self, preferred_element_type=jnp.float32) + jnp.dot(mean_rows, w_neigh, preferred_element_type=jnp.float32)
        hid = jax.nn.silu(pre).astype(jnp.bfloat16)
        grad_pre = (ct.astype(jnp.float32) * silu_slope(pre)).astype(jnp.bfloat16)
        part_self = lax.dot_general(block, grad_pre, contract, preferred_element_type=jnp.float32)
        part_neigh = lax.dot_general(mean_rows, grad_pre, contract, preferred_element_type=jnp.float32)
        grad_mean = lax.dot_general(grad_pre, w_neigh, trans, preferred_element_type=jnp.float32) / FAN
        spread = jnp.broadcast_to(grad_mean[:, None, :], (ROWS, FAN, D_IN)).reshape(ROWS * FAN, D_IN)
        grad_table = jnp.zeros((ROWS + ROUNDS * CAP, D_IN), jnp.float32).at[nb.reshape(-1)].add(spread)
        own = lax.dot_general(grad_pre, w_self, trans, preferred_element_type=jnp.float32) + grad_table[:ROWS]
        return hid, part_self, part_neigh, own, grad_table[ROWS:].reshape(ROUNDS, CAP, D_IN)

    hid, part_self, part_neigh, own, grad_halo = lax.map(forward, (feat, received, nbr, cot))
    returned = grad_halo[partner, round_ids[None, :]] * live[:, :, :, None]

    def settle(args):
        grads, rows_sent, back = args
        return grads.at[rows_sent.reshape(-1)].add(back.reshape(ROUNDS * CAP, D_IN))

    grad_feat = lax.map(settle, (own, send_rows, returned))
    scale = jnp.float32(NODES) ** -0.5
    return (hid.reshape(NODES, HID), grad_feat.reshape(NODES, D_IN),
            jnp.sum(part_self, axis=0) * scale, jnp.sum(part_neigh, axis=0) * scale)
```

```python
import functools

import jax
import jax.numpy as jnp
from jax import lax
from jax.experimental import pallas as pl
from jax.experimental.pallas import tpu as pltpu
from jax.sharding import PartitionSpec as P

FAN = 10
ROUNDS = 5
CAP = 256
ROWS = 2048
EXT = ROWS + ROUNDS * CAP
D = 128
H = 256
GROUP = 32
ZS = 8
WORDS = 8
DIGITS = 7
MESH = pl.DeviceIdType.MESH
f32, bf16, i32 = jnp.float32, jnp.bfloat16, jnp.int32
ORDER = (3, 2, 4, 1, 0)


def partner_of(me, b):
    bit = (me // 2**b) % 2
    return me + (1 - 2 * bit) * 2**b


def build_counts(l, nbt_ref, val_ref, ct_ref):
    nb = nbt_ref[:, pl.ds(l, 128)]
    one = jnp.int32(1) << (4 * (nb >> 9))
    group = (nb >> 6) & 7
    val_ref[0] = nb & 63
    for q in range(WORDS):
        val_ref[1 + q] = jnp.where(group == q, one, 0)
    for half in range(2):
        rid = lax.broadcasted_iota(i32, (32, 128), 0) + 32 * half
        acc = [jnp.zeros((32, 128), i32)] * WORDS
        for k in range(FAN):
            hit = val_ref[0, k : k + 1, :] == rid
            for q in range(WORDS):
                acc[q] = acc[q] + jnp.where(hit, val_ref[1 + q, k : k + 1, :], 0)
        for q in range(WORDS):
            for s in range(DIGITS):
                row = s * 512 + q * 64 + half * 32
                if row < EXT:
                    digit = acc[q] & jnp.int32(15 << (4 * s))
                    ct_ref[row : row + 32, pl.ds(l, 128)] = digit.astype(f32).astype(bf16)


def kernel(
    feat_hbm, ws_ref, wn_ref, cot_hbm, nbt_ref, key_ref,
    hid_hbm, gf_hbm, gws_ref, gwn_ref,
    ct, pt, fv, xt, tt, cotv, gp, hidv, gm, own, hs, hr, bs, br,
    wcat, wt, val, gw, gwc, rsr, zr, agr,
    in_sem, out_sem, hs_s, hs_r, bs_s, bs_r, rs_s, rs_r, z_s, z_r, ag_s, ag_r,
):
    me = lax.axis_index("dom")
    core = me % 2
    z = (me // 2) % ZS
    xy = me // (2 * ZS)
    m = xy * 2 + core

    def member(mm):
        return (mm // 2) * (2 * ZS) + z * 2 + mm % 2

    def at_z(zz):
        return xy * (2 * ZS) + zz * 2 + core

    get_feat = pltpu.make_async_copy(feat_hbm, fv, in_sem.at[0])
    get_cot = pltpu.make_async_copy(cot_hbm, cotv, in_sem.at[1])
    get_feat.start()
    get_cot.start()

    barrier = pltpu.get_barrier_semaphore()

    def greet(j, c):
        pl.semaphore_signal(barrier, inc=1, device_id=(member((m + j) % GROUP),), device_id_type=MESH)
        return c

    lax.fori_loop(1, GROUP, greet, 0)

    def greet_z(j, c):
        pl.semaphore_signal(barrier, inc=1, device_id=(at_z((z + j) % ZS),), device_id_type=MESH)
        return c

    lax.fori_loop(1, ZS, greet_z, 0)

    wcat[0:D, :] = ws_ref[...]
    wcat[D : 2 * D, :] = wn_ref[...]
    wt[:, 0:D] = wn_ref[...].T
    wt[:, D : 2 * D] = ws_ref[...].T
    get_feat.wait()
    for s in range(4):
        piece = fv[512 * s : 512 * (s + 1), :].T
        xt[0:D, 512 * s : 512 * (s + 1)] = piece
        tt[:, 512 * s : 512 * (s + 1)] = piece * jnp.bfloat16(16.0**-s)

    def halo(b):
        return pltpu.make_async_remote_copy(
            src_ref=hs.at[b], dst_ref=hr.at[b], send_sem=hs_s.at[b], recv_sem=hs_r.at[b],
            device_id=(partner_of(me, b),), device_id_type=MESH)

    for at, b in enumerate(ORDER):
        def pick(i, c, b=b):
            r = pl.multiple_of(i * 256, 256)
            ids = lax.broadcasted_iota(i32, (256, CAP), 0) + r
            hit = key_ref[b : b + 1, :] == ids
            pt[pl.ds(r, 256), b * CAP : (b + 1) * CAP] = jnp.where(hit, 1.0, 0.0).astype(bf16)
            return c

        lax.fori_loop(0, ROWS // 256, pick, 0)
        hs[b] = jnp.dot(
            xt[0:D, :], pt[:, b * CAP : (b + 1) * CAP], preferred_element_type=f32).astype(bf16)
        if at == 0:
            pl.semaphore_wait(barrier, GROUP - 1 + ZS - 1)
        halo(b).start()

    def build(i, c):
        build_counts(pl.multiple_of(i * 128, 128), nbt_ref, val, ct)
        return c

    lax.fori_loop(0, ROWS // 128, build, 0)

    for b in ORDER:
        halo(b).wait()
        s = (ROWS + b * CAP) // 512
        tt[:, ROWS + b * CAP : ROWS + (b + 1) * CAP] = hr[b] * jnp.bfloat16(16.0**-s)

    get_cot.wait()
    NB = 512

    def put_hid(i):
        return pltpu.make_async_copy(
            hidv.at[pl.ds(i * NB, NB)], hid_hbm.at[pl.ds(i * NB, NB)], out_sem.at[i])

    def dense(i, c):
        l = pl.multiple_of(i * NB, NB)
        total = jnp.dot(tt[...], ct[:, pl.ds(l, NB)], preferred_element_type=f32)
        mean_t = (total * (1.0 / FAN)).astype(bf16)
        xt[D : 2 * D, pl.ds(l, NB)] = mean_t
        x = jnp.concatenate([fv[pl.ds(l, NB), :], mean_t.T], axis=1)
        pre = jnp.dot(x, wcat[...], preferred_element_type=f32)
        sig = 1.0 / (1.0 + jnp.exp(-pre))
        hidv[pl.ds(l, NB), :] = (pre * sig).astype(bf16)
        slope = sig * (1.0 + pre * (1.0 - sig))
        grad = (cotv[pl.ds(l, NB), :].astype(f32) * slope).astype(bf16)
        gp[pl.ds(l, NB), :] = grad
        both = jnp.dot(grad, wt[...], preferred_element_type=f32)
        gm[pl.ds(l, NB), :] = (both[:, 0:D] * (1.0 / FAN)).astype(bf16)
        own[pl.ds(l, NB), :] = both[:, D : 2 * D]
        return c

    lax.fori_loop(0, ROWS // NB, dense, 0)
    for i in range(ROWS // NB):
        put_hid(i).start()

    gw[...] = jnp.dot(xt[...], gp[...], preferred_element_type=f32)
    for c in range(GROUP):
        gwc[c] = jnp.concatenate([gw[8 * c : 8 * c + 8, 0:D], gw[8 * c : 8 * c + 8, D:H]], axis=0).astype(bf16)

    def rs(j):
        to = (m + j) % GROUP
        return pltpu.make_async_remote_copy(
            src_ref=gwc.at[to], dst_ref=rsr.at[j], send_sem=rs_s.at[j], recv_sem=rs_r.at[j],
            device_id=(member(to),), device_id_type=MESH)

    def rs_start(j, c):
        rs(j).start()
        return c

    lax.fori_loop(1, GROUP, rs_start, 0)

    def back(b):
        return pltpu.make_async_remote_copy(
            src_ref=bs.at[b], dst_ref=br.at[pl.ds(b * CAP, CAP)], send_sem=bs_s.at[b], recv_sem=bs_r.at[b],
            device_id=(partner_of(me, b),), device_id_type=MESH)

    for b in ORDER:
        row = ROWS + b * CAP
        g = jnp.dot(ct[row : row + CAP, :], gm[...], preferred_element_type=f32)
        bs[b] = (g * (16.0 ** -(row // 512))).astype(bf16)
        back(b).start()

    rsr[0] = gwc[m]

    def rs_wait(j, c):
        rs(j).wait()
        return c

    lax.fori_loop(1, GROUP, rs_wait, 0)
    part = rsr[0].astype(f32)
    for j in range(1, GROUP):
        part = part + rsr[j].astype(f32)
    zr[z] = part

    def zx(j):
        return pltpu.make_async_remote_copy(
            src_ref=zr.at[z], dst_ref=zr.at[z], send_sem=z_s.at[j], recv_sem=z_r.at[j],
            device_id=(at_z((z + j) % ZS),), device_id_type=MESH)

    def z_start(j, c):
        zx(j).start()
        return c

    lax.fori_loop(1, ZS, z_start, 0)

    def local_back(s):
        g = jnp.dot(ct[512 * s : 512 * (s + 1), :], gm[...], preferred_element_type=f32)
        own[512 * s : 512 * (s + 1), :] += g * (16.0**-s)

    local_back(0)
    local_back(1)

    def z_wait(j, c):
        zx(j).wait_send()
        frm = (z + ZS - j) % ZS
        pltpu.make_async_remote_copy(
            src_ref=zr.at[z], dst_ref=zr.at[frm], send_sem=z_s.at[j], recv_sem=z_r.at[j],
            device_id=(at_z(frm),), device_id_type=MESH).wait_recv()
        return c

    lax.fori_loop(1, ZS, z_wait, 0)
    full = zr[0]
    for j in range(1, ZS):
        full = full + zr[j]
    agr[m] = (full * (2.0**-9.5)).astype(bf16)

    def ag(j):
        return pltpu.make_async_remote_copy(
            src_ref=agr.at[m], dst_ref=agr.at[m], send_sem=ag_s.at[j], recv_sem=ag_r.at[j],
            device_id=(member((m + j) % GROUP),), device_id_type=MESH)

    def ag_start(j, c):
        ag(j).start()
        return c

    lax.fori_loop(1, GROUP, ag_start, 0)
    local_back(2)
    local_back(3)

    for b in ORDER:
        back(b).wait()

    def put_gf(i):
        return pltpu.make_async_copy(
            own.at[pl.ds(i * NB, NB)], gf_hbm.at[pl.ds(i * NB, NB)], out_sem.at[4 + i])

    for i in range(ROWS // NB):
        own[NB * i : NB * (i + 1), :] += jnp.dot(
            pt[NB * i : NB * (i + 1), :], br[...], preferred_element_type=f32)
        put_gf(i).start()

    def ag_wait(j, c):
        ag(j).wait_send()
        frm = (m + GROUP - j) % GROUP
        pltpu.make_async_remote_copy(
            src_ref=agr.at[m], dst_ref=agr.at[frm], send_sem=ag_s.at[j], recv_sem=ag_r.at[j],
            device_id=(member(frm),), device_id_type=MESH).wait_recv()
        return c

    lax.fori_loop(1, GROUP, ag_wait, 0)
    for c in range(GROUP):
        chunk = agr[c].astype(f32)
        ref = gws_ref if c < 16 else gwn_ref
        r = 8 * (c % 16)
        ref[r : r + 8, 0:D] = chunk[0:8]
        ref[r : r + 8, D:H] = chunk[8:16]
    for i in range(ROWS // NB):
        put_hid(i).wait()
        put_gf(i).wait()


def on_device(features, w_self, w_neigh, cotangent, neighbours, send_rows, send_count):
    slot = jnp.arange(CAP, dtype=i32)
    key = jnp.where(slot[None, :] < send_count[0][:, None], send_rows[0], -1)
    vmem = pl.BlockSpec(memory_space=pltpu.VMEM)
    hbm = pl.BlockSpec(memory_space=pl.ANY)
    dma = pltpu.SemaphoreType.DMA
    call = pl.pallas_call(
        kernel,
        out_shape=(
            jax.ShapeDtypeStruct((ROWS, H), bf16),
            jax.ShapeDtypeStruct((ROWS, D), f32),
            jax.ShapeDtypeStruct((D, H), f32),
            jax.ShapeDtypeStruct((D, H), f32),
        ),
        in_specs=[hbm, vmem, vmem, hbm, vmem, vmem],
        out_specs=(hbm, hbm, vmem, vmem),
        scratch_shapes=[
            pltpu.VMEM((EXT, ROWS), bf16),
            pltpu.VMEM((ROWS, ROUNDS * CAP), bf16),
            pltpu.VMEM((ROWS, D), bf16),
            pltpu.VMEM((2 * D, ROWS), bf16),
            pltpu.VMEM((D, EXT), bf16),
            pltpu.VMEM((ROWS, H), bf16),
            pltpu.VMEM((ROWS, H), bf16),
            pltpu.VMEM((ROWS, H), bf16),
            pltpu.VMEM((ROWS, D), bf16),
            pltpu.VMEM((ROWS, D), f32),
            pltpu.VMEM((ROUNDS, D, CAP), bf16),
            pltpu.VMEM((ROUNDS, D, CAP), bf16),
            pltpu.VMEM((ROUNDS, CAP, D), bf16),
            pltpu.VMEM((ROUNDS * CAP, D), bf16),
            pltpu.VMEM((2 * D, H), bf16),
            pltpu.VMEM((H, 2 * D), bf16),
            pltpu.VMEM((1 + WORDS, FAN, 128), i32),
            pltpu.VMEM((2 * D, H), f32),
            pltpu.VMEM((GROUP, 16, D), bf16),
            pltpu.VMEM((GROUP, 16, D), bf16),
            pltpu.VMEM((ZS, 16, D), f32),
            pltpu.VMEM((GROUP, 16, D), bf16),
            dma((2,)), dma((8,)),
            dma((ROUNDS,)), dma((ROUNDS,)), dma((ROUNDS,)), dma((ROUNDS,)),
            dma((GROUP,)), dma((GROUP,)), dma((ZS,)), dma((ZS,)), dma((GROUP,)), dma((GROUP,)),
        ],
        compiler_params=pltpu.CompilerParams(
            collective_id=0, has_side_effects=True, vmem_limit_bytes=48 * 1024 * 1024),
        cost_estimate=pl.CostEstimate(flops=4_500_000_000, bytes_accessed=6_000_000, transcendentals=1_000_000),
    )
    return call(features, w_self, w_neigh, cotangent, neighbours.T, key)


def solution(mesh):
    placed = (
        P("dom", None), P(), P(), P("dom", None), P("dom", None), P("dom", None, None), P("dom", None),
    )
    return jax.shard_map(
        on_device,
        mesh=mesh,
        in_specs=placed,
        out_specs=(P("dom", None), P("dom", None), P(), P()),
        check_vma=False,
    )
```

```python
import functools

import jax
import jax.numpy as jnp
from jax import lax
from jax.experimental import pallas as pl
from jax.experimental.pallas import tpu as pltpu
from jax.sharding import PartitionSpec as P

FAN = 10
ROUNDS = 5
CAP = 256
ROWS = 2048
HALF = ROWS // 2
EXT = ROWS + ROUNDS * CAP
D = 128
H = 256
GROUP = 32
ZS = 8
WORDS = 8
DIGITS = 7
MESH = pl.DeviceIdType.MESH
f32, bf16, i32 = jnp.float32, jnp.bfloat16, jnp.int32
ORDER = (3, 2, 4, 1, 0)
STEPS = sorted(
    ((dy, dx, dc) for dy in range(4) for dx in range(4) for dc in range(2)),
    key=lambda step: (step == (0, 0, 0), min(step[0], 4 - step[0]) + min(step[1], 4 - step[1])),
    reverse=True,
)


def partner_of(me, b):
    bit = (me // 2**b) % 2
    return me + (1 - 2 * bit) * 2**b


def build_counts(l, to, nbt_ref, val_ref, ct_ref):
    nb = nbt_ref[:, pl.ds(l, 128)]
    one = jnp.int32(1) << (4 * (nb >> 9))
    group = (nb >> 6) & 7
    val_ref[0] = nb & 63
    for q in range(WORDS):
        val_ref[1 + q] = jnp.where(group == q, one, 0)
    for half in range(2):
        rid = lax.broadcasted_iota(i32, (32, 128), 0) + 32 * half
        acc = [jnp.zeros((32, 128), i32)] * WORDS
        for k in range(FAN):
            hit = val_ref[0, k : k + 1, :] == rid
            for q in range(WORDS):
                acc[q] = acc[q] + jnp.where(hit, val_ref[1 + q, k : k + 1, :], 0)
        for q in range(WORDS):
            for s in range(DIGITS):
                row = s * 512 + q * 64 + half * 32
                if row < EXT:
                    digit = acc[q] & jnp.int32(15 << (4 * s))
                    ct_ref[row : row + 32, pl.ds(to, 128)] = digit.astype(f32).astype(bf16)


def kernel(
    feat_hbm, ws_hbm, wn_hbm, cot_hbm, nbt_hbm, rows_hbm, live_hbm,
    hidv, own, gws_ref, gwn_ref,
    ws_ref, wn_ref, nbt_ref, rows_ref, live_ref, stl, cta, ctb, pt, fv, xt, tt, cotv, gp, gm, hs, hr, bs, br,
    wcat, wt, val, valb, gw, gwc, rsr, zr, agr,
    in_sem, hs_s, hs_r, bs_s, bs_r, rs_s, rs_r, z_s, z_r, ag_s, ag_r,
):
    me = lax.axis_index("dom")
    core = me % 2
    z = (me // 2) % ZS
    xy = me // (2 * ZS)
    m = xy * 2 + core

    def member(mm):
        return (mm // 2) * (2 * ZS) + z * 2 + mm % 2

    def plane(step):
        dy, dx, dc = step
        return ((xy // 4 + dy) % 4) * 8 + ((xy % 4 + dx) % 4) * 2 + (core + dc) % 2

    def at_z(zz):
        return xy * (2 * ZS) + zz * 2 + core

    fetch = [
        pltpu.make_async_copy(src, dst, in_sem.at[i])
        for i, (src, dst) in enumerate((
            (rows_hbm, rows_ref), (live_hbm, live_ref), (feat_hbm, fv), (nbt_hbm, nbt_ref),
            (ws_hbm, ws_ref), (wn_hbm, wn_ref), (cot_hbm, cotv)))
    ]
    for one in fetch:
        one.start()

    barrier = pltpu.get_barrier_semaphore()

    def greet(j, c):
        pl.semaphore_signal(barrier, inc=1, device_id=(member((m + j) % GROUP),), device_id_type=MESH)
        return c

    lax.fori_loop(1, GROUP, greet, 0)

    def greet_z(j, c):
        pl.semaphore_signal(barrier, inc=1, device_id=(at_z((z + j) % ZS),), device_id_type=MESH)
        return c

    lax.fori_loop(1, ZS, greet_z, 0)

    fetch[0].wait()
    fetch[1].wait()
    fetch[2].wait()
    for s in range(4):
        piece = fv[512 * s : 512 * (s + 1), :].T
        xt[0:D, 512 * s : 512 * (s + 1)] = piece
        tt[:, 512 * s : 512 * (s + 1)] = piece * jnp.bfloat16(16.0**-s)

    def halo(b):
        return pltpu.make_async_remote_copy(
            src_ref=hs.at[b], dst_ref=hr.at[b], send_sem=hs_s.at[b], recv_sem=hs_r.at[b],
            device_id=(partner_of(me, b),), device_id_type=MESH)

    for at, b in enumerate(ORDER):
        slot = lax.broadcasted_iota(i32, (1, CAP), 1)
        key = jnp.where(slot < live_ref[0:1, b : b + 1], rows_ref[b], -1)

        def pick(i, c, b=b, key=key):
            r = pl.multiple_of(i * 256, 256)
            ids = lax.broadcasted_iota(i32, (256, CAP), 0) + r
            hit = key == ids
            pt[pl.ds(r, 256), b * CAP : (b + 1) * CAP] = jnp.where(hit, 1.0, 0.0).astype(bf16)
            return c

        lax.fori_loop(0, ROWS // 256, pick, 0)
        hs[b] = jnp.dot(
            xt[0:D, :], pt[:, b * CAP : (b + 1) * CAP], preferred_element_type=f32).astype(bf16)
        if at == 0:
            pl.semaphore_wait(barrier, GROUP - 1 + ZS - 1)
        halo(b).start()

    fetch[3].wait()

    def build_a(i):
        build_counts(pl.multiple_of(i * 128, 128), pl.multiple_of(i * 128, 128), nbt_ref, val, cta)

    def build_b(i):
        build_counts(pl.multiple_of(HALF + i * 128, 128), pl.multiple_of(i * 128, 128), nbt_ref, valb, ctb)

    def sum_own(i, base, ref):
        l = pl.multiple_of(i * 128, 128)
        stl[:, pl.ds(pl.multiple_of(base + i * 128, 128), 128)] = jnp.dot(
            tt[:, 0:ROWS], ref[0:ROWS, pl.ds(l, 128)], preferred_element_type=f32)

    build_a(0)

    def build(i, c):
        sum_own(i, 0, cta)
        build_b(i)
        sum_own(i, HALF, ctb)
        build_a(i + 1)
        return c

    lax.fori_loop(0, HALF // 128 - 1, build, 0)
    sum_own(HALF // 128 - 1, 0, cta)
    build_b(HALF // 128 - 1)
    sum_own(HALF // 128 - 1, HALF, ctb)

    for i in (4, 5, 6):
        fetch[i].wait()
    wcat[0:D, :] = ws_ref[...]
    wcat[D : 2 * D, :] = wn_ref[...]
    wt[:, 0:D] = wn_ref[...].T
    wt[:, D : 2 * D] = ws_ref[...].T

    for b in ORDER:
        halo(b).wait()
        s = (ROWS + b * CAP) // 512
        tt[:, ROWS + b * CAP : ROWS + (b + 1) * CAP] = hr[b] * jnp.bfloat16(16.0**-s)

    NB = 512
    for i in range(ROWS // NB):
        l = i * NB
        ref = cta if l < HALF else ctb
        total = stl[:, l : l + NB] + jnp.dot(
            tt[:, ROWS:EXT], ref[ROWS:EXT, l % HALF : l % HALF + NB], preferred_element_type=f32)
        mean_t = (total * (1.0 / FAN)).astype(bf16)
        xt[D : 2 * D, l : l + NB] = mean_t
        x = jnp.concatenate([fv[l : l + NB, :], mean_t.T], axis=1)
        pre = jnp.dot(x, wcat[...], preferred_element_type=f32)
        sig = 0.5 + 0.5 * jnp.tanh(0.5 * pre)
        hidv[l : l + NB, :] = (pre * sig).astype(bf16)
        slope = sig * (1.0 + pre * (1.0 - sig))
        grad = (cotv[l : l + NB, :].astype(f32) * slope).astype(bf16)
        gp[l : l + NB, :] = grad
        both = jnp.dot(grad, wt[...], preferred_element_type=f32)
        gm[l : l + NB, :] = (both[:, 0:D] * (1.0 / FAN)).astype(bf16)
        own[l : l + NB, :] = both[:, D : 2 * D]

    gw[...] = jnp.dot(xt[...], gp[...], preferred_element_type=f32)
    for c in range(GROUP):
        gwc[c] = jnp.concatenate([gw[8 * c : 8 * c + 8, 0:D], gw[8 * c : 8 * c + 8, D:H]], axis=0).astype(bf16)

    def rs(j):
        to = plane(STEPS[j])
        return pltpu.make_async_remote_copy(
            src_ref=gwc.at[to], dst_ref=rsr.at[j], send_sem=rs_s.at[j], recv_sem=rs_r.at[j],
            device_id=(member(to),), device_id_type=MESH)

    for j in range(1, GROUP):
        rs(j).start()

    def spread(row, count):
        return jnp.dot(
            cta[row : row + count, :], gm[0:HALF, :], preferred_element_type=f32
        ) + jnp.dot(ctb[row : row + count, :], gm[HALF:ROWS, :], preferred_element_type=f32)

    def back(b):
        return pltpu.make_async_remote_copy(
            src_ref=bs.at[b], dst_ref=br.at[pl.ds(b * CAP, CAP)], send_sem=bs_s.at[b], recv_sem=bs_r.at[b],
            device_id=(partner_of(me, b),), device_id_type=MESH)

    for b in ORDER:
        row = ROWS + b * CAP
        g = spread(row, CAP)
        bs[b] = (g * (16.0 ** -(row // 512))).astype(bf16)
        back(b).start()

    rsr[0] = gwc[m]

    for j in range(1, GROUP):
        rs(j).wait()
    part = rsr[0].astype(f32)
    for j in range(1, GROUP):
        part = part + rsr[j].astype(f32)
    zr[z] = part

    def zx(j):
        return pltpu.make_async_remote_copy(
            src_ref=zr.at[z], dst_ref=zr.at[z], send_sem=z_s.at[j], recv_sem=z_r.at[j],
            device_id=(at_z((z + j) % ZS),), device_id_type=MESH)

    for j in (4, 3, 5, 2, 6, 1, 7):
        zx(j).start()

    def local_back(s):
        g = spread(512 * s, 512)
        own[512 * s : 512 * (s + 1), :] += g * (16.0**-s)

    local_back(0)
    local_back(1)

    def z_wait(j):
        zx(j).wait_send()
        frm = (z + ZS - j) % ZS
        pltpu.make_async_remote_copy(
            src_ref=zr.at[z], dst_ref=zr.at[frm], send_sem=z_s.at[j], recv_sem=z_r.at[j],
            device_id=(at_z(frm),), device_id_type=MESH).wait_recv()

    for j in range(1, ZS):
        z_wait(j)
    full = zr[0]
    for j in range(1, ZS):
        full = full + zr[j]
    agr[m] = (full * (2.0**-9.5)).astype(bf16)

    def ag(j):
        return pltpu.make_async_remote_copy(
            src_ref=agr.at[m], dst_ref=agr.at[m], send_sem=ag_s.at[j], recv_sem=ag_r.at[j],
            device_id=(member(plane(STEPS[j])),), device_id_type=MESH)

    for j in range(1, GROUP):
        ag(j).start()
    local_back(2)
    local_back(3)

    for b in ORDER:
        back(b).wait()

    for i in range(ROWS // NB):
        own[NB * i : NB * (i + 1), :] += jnp.dot(
            pt[NB * i : NB * (i + 1), :], br[...], preferred_element_type=f32)

    def ag_wait(j):
        ag(j).wait_send()
        dy, dx, dc = STEPS[j]
        frm = plane((4 - dy, 4 - dx, 2 - dc))
        pltpu.make_async_remote_copy(
            src_ref=agr.at[m], dst_ref=agr.at[frm], send_sem=ag_s.at[j], recv_sem=ag_r.at[j],
            device_id=(member(frm),), device_id_type=MESH).wait_recv()

    for j in range(1, GROUP):
        ag_wait(j)
    for c in range(GROUP):
        chunk = agr[c].astype(f32)
        ref = gws_ref if c < 16 else gwn_ref
        r = 8 * (c % 16)
        ref[r : r + 8, 0:D] = chunk[0:8]
        ref[r : r + 8, D:H] = chunk[8:16]


def hand_over(hid, gf, gws, gwn, hid_out, gf_out, gws_out, gwn_out, sem):
    copies = [
        pltpu.make_async_copy(src, dst, sem.at[i])
        for i, (src, dst) in enumerate(((hid, hid_out), (gf, gf_out), (gws, gws_out), (gwn, gwn_out)))
    ]
    for one in copies:
        one.start()
    for one in copies:
        one.wait()


def on_device(features, w_self, w_neigh, cotangent, neighbours, send_rows, send_count):
    vmem = pl.BlockSpec(memory_space=pltpu.VMEM)
    hbm = pl.BlockSpec(memory_space=pl.ANY)
    dma = pltpu.SemaphoreType.DMA
    shapes = (((ROWS, H), bf16), ((ROWS, D), f32), ((D, H), f32), ((D, H), f32))
    call = pl.pallas_call(
        kernel,
        out_shape=tuple(pltpu.VMEM(*one) for one in shapes),
        in_specs=[hbm] * 7,
        out_specs=(vmem,) * 4,
        scratch_shapes=[
            pltpu.VMEM((D, H), bf16),
            pltpu.VMEM((D, H), bf16),
            pltpu.VMEM((FAN, ROWS), i32),
            pltpu.VMEM((ROUNDS, 1, CAP), i32),
            pltpu.VMEM((1, ROUNDS), i32),
            pltpu.VMEM((D, ROWS), f32),
            pltpu.VMEM((EXT, HALF), bf16),
            pltpu.VMEM((EXT, HALF), bf16),
            pltpu.VMEM((ROWS, ROUNDS * CAP), bf16),
            pltpu.VMEM((ROWS, D), bf16),
            pltpu.VMEM((2 * D, ROWS), bf16),
            pltpu.VMEM((D, EXT), bf16),
            pltpu.VMEM((ROWS, H), bf16),
            pltpu.VMEM((ROWS, H), bf16),
            pltpu.VMEM((ROWS, D), bf16),
            pltpu.VMEM((ROUNDS, D, CAP), bf16),
            pltpu.VMEM((ROUNDS, D, CAP), bf16),
            pltpu.VMEM((ROUNDS, CAP, D), bf16),
            pltpu.VMEM((ROUNDS * CAP, D), bf16),
            pltpu.VMEM((2 * D, H), bf16),
            pltpu.VMEM((H, 2 * D), bf16),
            pltpu.VMEM((1 + WORDS, FAN, 128), i32),
            pltpu.VMEM((1 + WORDS, FAN, 128), i32),
            pltpu.VMEM((2 * D, H), f32),
            pltpu.VMEM((GROUP, 16, D), bf16),
            pltpu.VMEM((GROUP, 16, D), bf16),
            pltpu.VMEM((ZS, 16, D), f32),
            pltpu.VMEM((GROUP, 16, D), bf16),
            dma((7,)),
            dma((ROUNDS,)), dma((ROUNDS,)), dma((ROUNDS,)), dma((ROUNDS,)),
            dma((GROUP,)), dma((GROUP,)), dma((ZS,)), dma((ZS,)), dma((GROUP,)), dma((GROUP,)),
        ],
        compiler_params=pltpu.CompilerParams(
            collective_id=0, has_side_effects=True, vmem_limit_bytes=48 * 1024 * 1024),
        cost_estimate=pl.CostEstimate(flops=4_500_000_000, bytes_accessed=6_000_000, transcendentals=1_000_000),
    )
    args = (features, w_self, w_neigh, cotangent, neighbours.T, send_rows.reshape(ROUNDS, 1, CAP), send_count)
    args = tuple(pltpu.with_memory_space_constraint(one, pltpu.HBM) for one in args)
    return pl.pallas_call(
        hand_over,
        out_shape=tuple(pltpu.HBM(*one) for one in shapes),
        in_specs=[vmem] * 4,
        out_specs=(hbm,) * 4,
        scratch_shapes=[dma((4,))],
    )(*[pltpu.with_memory_space_constraint(one, pltpu.VMEM) for one in call(*args)])


def solution(mesh):
    placed = (
        P("dom", None), P(), P(), P("dom", None), P("dom", None), P("dom", None, None), P("dom", None),
    )
    return jax.shard_map(
        on_device,
        mesh=mesh,
        in_specs=placed,
        out_specs=(P("dom", None), P("dom", None), P(), P()),
        check_vma=False,
    )
```

```python
import functools

import jax
import jax.numpy as jnp
from jax import lax
from jax.experimental import pallas as pl
from jax.experimental.pallas import tpu as pltpu
from jax.sharding import PartitionSpec as P

FAN = 10
ROUNDS = 5
CAP = 256
ROWS = 2048
EXT = ROWS + ROUNDS * CAP
D = 128
H = 256
GROUP = 32
ZS = 8
WORDS = 8
DIGITS = 7
MESH = pl.DeviceIdType.MESH
f32, bf16, i32 = jnp.float32, jnp.bfloat16, jnp.int32
ORDER = (3, 2, 1, 4, 0)


def ring(step, size):
    return min(step, size - step)


PLANE = sorted(
    ((dy, dx, dc) for dy in range(4) for dx in range(4) for dc in range(2)),
    key=lambda t: (t != (0, 0, 0), ring(t[0], 4) + ring(t[1], 4)), reverse=True)
LINE = sorted(range(8), key=lambda t: (t != 0, ring(t, 8)), reverse=True)


def partner_of(me, b):
    bit = (me // 2**b) % 2
    return me + (1 - 2 * bit) * 2**b


def build_counts(l, nbt_ref, val_ref, ct_ref):
    nb = nbt_ref[:, pl.ds(l, 128)]
    one = jnp.int32(1) << (4 * (nb >> 9))
    group = (nb >> 6) & 7
    val_ref[0] = nb & 63
    for q in range(WORDS):
        val_ref[1 + q] = jnp.where(group == q, one, 0)
    for half in range(2):
        rid = lax.broadcasted_iota(i32, (32, 128), 0) + 32 * half
        acc = [jnp.zeros((32, 128), i32)] * WORDS
        for k in range(FAN):
            hit = val_ref[0, k : k + 1, :] == rid
            for q in range(WORDS):
                acc[q] = acc[q] + jnp.where(hit, val_ref[1 + q, k : k + 1, :], 0)
        for q in range(WORDS):
            for s in range(DIGITS):
                row = s * 512 + q * 64 + half * 32
                if row < EXT:
                    digit = acc[q] & jnp.int32(15 << (4 * s))
                    ct_ref[row : row + 32, pl.ds(l, 128)] = digit.astype(f32).astype(bf16)


def kernel(
    feat_hbm, ws_hbm, wn_hbm, cot_hbm, nbt_hbm, rows_hbm, live_hbm,
    hidv, own, gws_ref, gwn_ref,
    ws_ref, wn_ref, nbt_ref, rows_ref, live_ref, stl, ct, pt, fv, xt, tt, cotv, gp, gm, hs, hr, bs, br,
    wcat, wt, val, gw, gwc, rsr, zr, agr, rows_s, ff, picked,
    in_sem, hs_s, hs_r, bs_s, bs_r, rs_s, rs_r, z_s, z_r, ag_s, ag_r,
):
    me = lax.axis_index("dom")
    core = me % 2
    z = (me // 2) % 8
    x = (me // 16) % 4
    y = me // 64
    spot = (y * 4 + x) * 2 + core

    def plane(step, sign=1):
        there = ((y + sign * step[0] + 4) % 4) * 4 + (x + sign * step[1] + 4) % 4
        return there * 2 + (core + step[2]) % 2

    def line(step, sign=1):
        return (z + sign * step + ZS) % ZS

    def at_plane(place):
        return (place // 2) * 16 + z * 2 + place % 2

    def at_line(place):
        return (spot // 2) * 16 + place * 2 + core

    fetch = [
        pltpu.make_async_copy(src, dst, in_sem.at[i])
        for i, (src, dst) in enumerate((
            (rows_hbm, rows_ref), (live_hbm, live_ref), (feat_hbm, fv), (nbt_hbm, nbt_ref),
            (ws_hbm, ws_ref), (wn_hbm, wn_ref), (cot_hbm, cotv), (rows_hbm, rows_s)))
    ]
    for one in fetch:
        one.start()

    barrier = pltpu.get_barrier_semaphore()

    for j in range(GROUP - 1):
        pl.semaphore_signal(barrier, inc=1, device_id=(at_plane(plane(PLANE[j])),), device_id_type=MESH)
    for j in range(ZS - 1):
        pl.semaphore_signal(barrier, inc=1, device_id=(at_line(line(LINE[j])),), device_id_type=MESH)

    def halo(b):
        return pltpu.make_async_remote_copy(
            src_ref=hs.at[b], dst_ref=hr.at[b], send_sem=hs_s.at[b], recv_sem=hs_r.at[b],
            device_id=(partner_of(me, b),), device_id_type=MESH)

    fetch[2].wait()
    ff[...] = fv[...].astype(f32)
    for i in (0, 1, 7):
        fetch[i].wait()
    for at, b in enumerate(ORDER):
        def load(i, c, b=b):
            r = pl.multiple_of(i * 32, 32)
            for t in range(32):
                picked[pl.ds(r + t, 1), :] = ff[pl.ds(rows_s[b, 0, r + t], 1), :]
            return c

        lax.fori_loop(0, CAP // 32, load, 0)
        live = lax.broadcasted_iota(i32, (CAP, D), 0) < live_ref[0:1, b : b + 1]
        hs[b] = jnp.where(live, picked[...], 0.0).astype(bf16)
        if at == 0:
            pl.semaphore_wait(barrier, GROUP + ZS - 2)
        halo(b).start()

    for s in range(4):
        piece = fv[512 * s : 512 * (s + 1), :].T
        xt[0:D, 512 * s : 512 * (s + 1)] = piece
        tt[:, 512 * s : 512 * (s + 1)] = piece * jnp.bfloat16(16.0**-s)

    def owners(b):
        slot = lax.broadcasted_iota(i32, (1, CAP), 1)
        key = jnp.where(slot < live_ref[0:1, b : b + 1], rows_ref[b], -1)

        def pick(i, c):
            r = pl.multiple_of(i * 512, 512)
            hit = key == lax.broadcasted_iota(i32, (512, CAP), 0) + r
            pt[pl.ds(r, 512), b * CAP : (b + 1) * CAP] = jnp.where(hit, 1.0, 0.0).astype(bf16)
            return c

        lax.fori_loop(0, ROWS // 512, pick, 0)

    fetch[3].wait()

    def build(i, c):
        build_counts(pl.multiple_of(i * 128, 128), nbt_ref, val, ct)
        return c

    lax.fori_loop(0, ROWS // 128, build, 0)
    stl[...] = jnp.dot(tt[:, 0:ROWS], ct[0:ROWS, :], preferred_element_type=f32)

    for i in (4, 5, 6):
        fetch[i].wait()
    wcat[0:D, :] = ws_ref[...]
    wcat[D : 2 * D, :] = wn_ref[...]
    wt[:, 0:D] = wn_ref[...].T
    wt[:, D : 2 * D] = ws_ref[...].T

    for b in ORDER:
        halo(b).wait()
        s = (ROWS + b * CAP) // 512
        tt[:, ROWS + b * CAP : ROWS + (b + 1) * CAP] = hr[b].T * jnp.bfloat16(16.0**-s)

    total = stl[...] + jnp.dot(tt[:, ROWS:EXT], ct[ROWS:EXT, :], preferred_element_type=f32)
    xt[D : 2 * D, :] = (total * (1.0 / FAN)).astype(bf16)
    NB = 512

    def pre_of(i):
        l = i * NB
        both_in = jnp.concatenate([fv[l : l + NB, :], xt[D : 2 * D, l : l + NB].T], axis=1)
        return jnp.dot(both_in, wcat[...], preferred_element_type=f32)

    pre = pre_of(0)
    for i in range(ROWS // NB):
        l = i * NB
        later = pre_of(i + 1) if i + 1 < ROWS // NB else None
        sig = 0.5 + 0.5 * jnp.tanh(0.5 * pre)
        silu = pre * sig
        hidv[l : l + NB, :] = silu.astype(bf16)
        slope = sig + silu * (1.0 - sig)
        grad = (cotv[l : l + NB, :].astype(f32) * slope).astype(bf16)
        gp[l : l + NB, :] = grad
        both = jnp.dot(grad, wt[...], preferred_element_type=f32)
        gm[l : l + NB, :] = (both[:, 0:D] * (1.0 / FAN)).astype(bf16)
        own[l : l + NB, :] = both[:, D : 2 * D]
        pre = later

    gw[...] = jnp.dot(xt[...], gp[...], preferred_element_type=f32)
    for c in range(GROUP):
        r = 8 * c
        gwc[c] = jnp.concatenate([gw[r : r + 8, 0:D], gw[r : r + 8, D:H]], axis=0).astype(bf16)

    def rs(j):
        to = plane(PLANE[j])
        return pltpu.make_async_remote_copy(
            src_ref=gwc.at[to], dst_ref=rsr.at[j], send_sem=rs_s.at[j], recv_sem=rs_r.at[j],
            device_id=(at_plane(to),), device_id_type=MESH)

    for j in range(GROUP - 1):
        rs(j).start()

    def spread(row, count):
        return jnp.dot(ct[row : row + count, :], gm[...], preferred_element_type=f32)

    def back(b):
        return pltpu.make_async_remote_copy(
            src_ref=bs.at[b], dst_ref=br.at[pl.ds(b * CAP, CAP)], send_sem=bs_s.at[b], recv_sem=bs_r.at[b],
            device_id=(partner_of(me, b),), device_id_type=MESH)

    for b in ORDER:
        row = ROWS + b * CAP
        g = spread(row, CAP)
        bs[b] = (g * (16.0 ** -(row // 512))).astype(bf16)
        back(b).start()

    def local_back(s):
        own[512 * s : 512 * (s + 1), :] += spread(512 * s, 512) * (16.0**-s)

    local_back(0)
    for b in (0, 1, 2):
        owners(b)
    for j in range(GROUP - 1):
        rs(j).wait()
    part = gwc[spot].astype(f32)
    for j in range(GROUP - 1):
        part = part + rsr[j].astype(f32)
    zr[z] = part.astype(bf16)

    def zx(j):
        return pltpu.make_async_remote_copy(
            src_ref=zr.at[z], dst_ref=zr.at[z], send_sem=z_s.at[j], recv_sem=z_r.at[j],
            device_id=(at_line(line(LINE[j])),), device_id_type=MESH)

    for j in range(ZS - 1):
        zx(j).start()
    for s in (1, 2, 3):
        local_back(s)
    for b in (3, 4):
        owners(b)

    def z_wait(j):
        zx(j).wait_send()
        frm = line(LINE[j], -1)
        pltpu.make_async_remote_copy(
            src_ref=zr.at[z], dst_ref=zr.at[frm], send_sem=z_s.at[j], recv_sem=z_r.at[j],
            device_id=(at_line(frm),), device_id_type=MESH).wait_recv()

    for j in range(ZS - 1):
        z_wait(j)
    full = zr[0].astype(f32)
    for j in range(1, ZS):
        full = full + zr[j].astype(f32)
    agr[spot] = (full * (2.0**-9.5)).astype(bf16)

    def ag(j):
        return pltpu.make_async_remote_copy(
            src_ref=agr.at[spot], dst_ref=agr.at[spot], send_sem=ag_s.at[j], recv_sem=ag_r.at[j],
            device_id=(at_plane(plane(PLANE[j])),), device_id_type=MESH)

    for j in range(GROUP - 1):
        ag(j).start()

    for b in ORDER:
        back(b).wait()

    for i in range(ROWS // NB):
        own[NB * i : NB * (i + 1), :] += jnp.dot(
            pt[NB * i : NB * (i + 1), :], br[...], preferred_element_type=f32)

    def ag_wait(j):
        ag(j).wait_send()
        frm = plane(PLANE[j], -1)
        pltpu.make_async_remote_copy(
            src_ref=agr.at[spot], dst_ref=agr.at[frm], send_sem=ag_s.at[j], recv_sem=ag_r.at[j],
            device_id=(at_plane(frm),), device_id_type=MESH).wait_recv()

    for j in range(GROUP - 1):
        ag_wait(j)
    for c in range(GROUP):
        chunk = agr[c].astype(f32)
        ref = gws_ref if c < GROUP // 2 else gwn_ref
        r = 8 * (c % (GROUP // 2))
        ref[r : r + 8, 0:D] = chunk[0:8]
        ref[r : r + 8, D:H] = chunk[8:16]


def hand_over(hid, gf, gws, gwn, hid_out, gf_out, gws_out, gwn_out, sem):
    copies = [
        pltpu.make_async_copy(src, dst, sem.at[i])
        for i, (src, dst) in enumerate(((hid, hid_out), (gf, gf_out), (gws, gws_out), (gwn, gwn_out)))
    ]
    for one in copies:
        one.start()
    for one in copies:
        one.wait()


def on_device(features, w_self, w_neigh, cotangent, neighbours, send_rows, send_count):
    vmem = pl.BlockSpec(memory_space=pltpu.VMEM)
    hbm = pl.BlockSpec(memory_space=pl.ANY)
    dma = pltpu.SemaphoreType.DMA
    shapes = (((ROWS, H), bf16), ((ROWS, D), f32), ((D, H), f32), ((D, H), f32))
    call = pl.pallas_call(
        kernel,
        out_shape=tuple(pltpu.VMEM(*one) for one in shapes),
        in_specs=[hbm] * 7,
        out_specs=(vmem,) * 4,
        scratch_shapes=[
            pltpu.VMEM((D, H), bf16),
            pltpu.VMEM((D, H), bf16),
            pltpu.VMEM((FAN, ROWS), i32),
            pltpu.VMEM((ROUNDS, 1, CAP), i32),
            pltpu.VMEM((1, ROUNDS), i32),
            pltpu.VMEM((D, ROWS), f32),
            pltpu.VMEM((EXT, ROWS), bf16),
            pltpu.VMEM((ROWS, ROUNDS * CAP), bf16),
            pltpu.VMEM((ROWS, D), bf16),
            pltpu.VMEM((2 * D, ROWS), bf16),
            pltpu.VMEM((D, EXT), bf16),
            pltpu.VMEM((ROWS, H), bf16),
            pltpu.VMEM((ROWS, H), bf16),
            pltpu.VMEM((ROWS, D), bf16),
            pltpu.VMEM((ROUNDS, CAP, D), bf16),
            pltpu.VMEM((ROUNDS, CAP, D), bf16),
            pltpu.VMEM((ROUNDS, CAP, D), bf16),
            pltpu.VMEM((ROUNDS * CAP, D), bf16),
            pltpu.VMEM((2 * D, H), bf16),
            pltpu.VMEM((H, 2 * D), bf16),
            pltpu.VMEM((1 + WORDS, FAN, 128), i32),
            pltpu.VMEM((2 * D, H), f32),
            pltpu.VMEM((GROUP, 16, D), bf16),
            pltpu.VMEM((GROUP, 16, D), bf16),
            pltpu.VMEM((ZS, 16, D), bf16),
            pltpu.VMEM((GROUP, 16, D), bf16),
            pltpu.SMEM((ROUNDS, 1, CAP), i32),
            pltpu.VMEM((ROWS, D), f32),
            pltpu.VMEM((CAP, D), f32),
            dma((8,)),
            dma((ROUNDS,)), dma((ROUNDS,)), dma((ROUNDS,)), dma((ROUNDS,)),
            dma((GROUP,)), dma((GROUP,)), dma((ZS,)), dma((ZS,)), dma((GROUP,)), dma((GROUP,)),
        ],
        compiler_params=pltpu.CompilerParams(
            collective_id=0, has_side_effects=True, vmem_limit_bytes=48 * 1024 * 1024),
        cost_estimate=pl.CostEstimate(flops=4_500_000_000, bytes_accessed=6_000_000, transcendentals=1_000_000),
    )
    args = (features, w_self, w_neigh, cotangent, neighbours.T, send_rows.reshape(ROUNDS, 1, CAP), send_count)
    args = tuple(pltpu.with_memory_space_constraint(one, pltpu.HBM) for one in args)
    return pl.pallas_call(
        hand_over,
        out_shape=tuple(pltpu.HBM(*one) for one in shapes),
        in_specs=[vmem] * 4,
        out_specs=(hbm,) * 4,
        scratch_shapes=[dma((4,))],
    )(*[pltpu.with_memory_space_constraint(one, pltpu.VMEM) for one in call(*args)])


def solution(mesh):
    placed = (
        P("dom", None), P(), P(), P("dom", None), P("dom", None), P("dom", None, None), P("dom", None),
    )
    return jax.shard_map(
        on_device,
        mesh=mesh,
        in_specs=placed,
        out_specs=(P("dom", None), P("dom", None), P(), P()),
        check_vma=False,
    )
```

```python
import functools

import jax
import jax.numpy as jnp
from jax import lax
from jax.experimental import pallas as pl
from jax.experimental.pallas import tpu as pltpu
from jax.sharding import PartitionSpec as P

FAN = 10
ROUNDS = 5
CAP = 256
ROWS = 2048
EXT = ROWS + ROUNDS * CAP
D = 128
H = 256
GROUP = 16
ZS = 8
WORDS = 13
DIGITS = 8
SPAN = EXT // DIGITS
MESH = pl.DeviceIdType.MESH
f32, bf16, i32 = jnp.float32, jnp.bfloat16, jnp.int32
ORDER = (3, 2, 1, 4, 0)


def ring(step, size):
    return min(step, size - step)


PLANE = sorted(
    ((dy, dx) for dy in range(4) for dx in range(4)),
    key=lambda t: (t != (0, 0), ring(t[0], 4) + ring(t[1], 4)), reverse=True)
LINE = sorted(range(8), key=lambda t: (t != 0, ring(t, 8)), reverse=True)


def partner_of(me, b):
    bit = lax.rem(lax.div(me, 2**b), 2)
    return me + (1 - 2 * bit) * 2**b


def power(digit):
    return min(digit, 6)


def spans(start, stop):
    cuts = [start] + [d * SPAN for d in range(1, DIGITS) if start < d * SPAN < stop] + [stop]
    return [(lo - start, hi - start, 16.0 ** -power(lo // SPAN)) for lo, hi in zip(cuts[:-1], cuts[1:])]


def lane_scale(start, count):
    row = lax.broadcasted_iota(i32, (1, count), 1)
    out = jnp.zeros((1, count), f32)
    for lo, hi, factor in spans(start, start + count):
        out = jnp.where(row >= lo, factor, out)
    return out.astype(bf16)


def build_counts(l, nbt_ref, val_ref, ct_ref):
    nb = nbt_ref[:, pl.ds(l, 128)]
    digit = (nb * 2521) >> 20
    rest = nb - digit * SPAN
    one = jnp.int32(1) << (4 * digit)
    group = rest >> 5
    val_ref[0] = rest & 31
    for q in range(WORDS):
        val_ref[1 + q] = jnp.where(group == q, one, 0)
    for half in range(2):
        rid = lax.broadcasted_iota(i32, (16, 128), 0) + 16 * half
        acc = [jnp.zeros((16, 128), i32)] * WORDS
        for k in range(FAN):
            hit = val_ref[0, k : k + 1, :] == rid
            for q in range(WORDS):
                acc[q] = acc[q] + jnp.where(hit, val_ref[1 + q, k : k + 1, :], 0)
        for q in range(WORDS):
            for s in range(DIGITS):
                row = s * SPAN + q * 32 + half * 16
                word = acc[q] if s < 7 else lax.shift_right_logical(acc[q], jnp.int32(4))
                count = word & jnp.int32(15 << (4 * power(s)))
                ct_ref[row : row + 16, pl.ds(l, 128)] = count.astype(f32).astype(bf16)


def kernel(
    feat_hbm, ws_hbm, wn_hbm, cot_hbm, nbt_hbm, rows_hbm, live_hbm,
    hidv, own, gws_ref, gwn_ref,
    ws_ref, wn_ref, nbt_ref, rows_ref, live_ref, stl, ct, pt, fv, xt, tt, cotv, gm, hs, hr, bs, br,
    wcat, wt, val, gw, gwc, rsr, zr, pair, agr, rows_s, ff, picked,
    in_sem, hs_s, hs_r, bs_s, bs_r, rs_s, rs_r, z_s, z_r, pair_sem, ag_s, ag_r,
):
    fetch = [
        pltpu.make_async_copy(src, dst, in_sem.at[i])
        for i, (src, dst) in enumerate((
            (rows_hbm, rows_ref), (live_hbm, live_ref), (feat_hbm, fv), (nbt_hbm, nbt_ref),
            (ws_hbm, ws_ref), (wn_hbm, wn_ref), (cot_hbm, cotv), (rows_hbm, rows_s)))
    ]
    for i in (2, 7, 0, 1, 3, 4, 5, 6):
        fetch[i].start()

    me = lax.axis_index("dom")
    core = lax.rem(me, 2)
    z = lax.rem(lax.div(me, 2), ZS)
    x = lax.rem(lax.div(me, 16), 4)
    y = lax.div(me, 64)
    zs = [z] + [lax.rem(z + d, ZS) for d in range(1, ZS)]
    xs = [x] + [lax.rem(x + d, 4) for d in range(1, 4)]
    ys = [y] + [lax.rem(y + d, 4) for d in range(1, 4)]
    spot = y * 4 + x
    twin = me + 1 - 2 * core

    def turned(step, back):
        return ((4 - step[0]) % 4, (4 - step[1]) % 4) if back else step

    def at_plane(step, back=False):
        dy, dx = turned(step, back)
        return ys[dy] * 64 + xs[dx] * 16 + z * 2 + core

    def place(step, back=False):
        dy, dx = turned(step, back)
        return ys[dy] * 4 + xs[dx]

    def line(step, back=False):
        return zs[(ZS - step) % ZS if back else step]

    def at_line(step, back=False):
        return y * 64 + x * 16 + line(step, back) * 2 + core

    barrier = pltpu.get_barrier_semaphore()
    for step in LINE[:-1]:
        pl.semaphore_signal(barrier, inc=1, device_id=(at_line(step),), device_id_type=MESH)
    for step in PLANE[:-1]:
        pl.semaphore_signal(barrier, inc=1, device_id=(at_plane(step),), device_id_type=MESH)

    pl.semaphore_signal(barrier, inc=1, device_id=(twin,), device_id_type=MESH)

    def halo(b):
        return pltpu.make_async_remote_copy(
            src_ref=hs.at[b], dst_ref=hr.at[b], send_sem=hs_s.at[b], recv_sem=hs_r.at[b],
            device_id=(partner_of(me, b),), device_id_type=MESH)

    fetch[2].wait()
    ff[...] = fv[...].astype(f32)
    for i in (0, 1, 7):
        fetch[i].wait()
    for at, b in enumerate(ORDER):
        def load(i, c, b=b):
            r = pl.multiple_of(i * 128, 128)
            for t in range(128):
                picked[pl.ds(r + t, 1), :] = ff[pl.ds(rows_s[2 * b + i, 0, t], 1), :]
            return c

        lax.fori_loop(0, CAP // 128, load, 0)
        live = lax.broadcasted_iota(i32, (CAP, D), 0) < live_ref[0:1, b : b + 1]
        hs[b] = jnp.where(live, picked[...], 0.0).astype(bf16)
        if at == 0:
            pl.semaphore_wait(barrier, GROUP + ZS - 1)
        if b:
            halo(b).start()

    for s in range(4):
        piece = fv[512 * s : 512 * (s + 1), :].T
        xt[0:D, 512 * s : 512 * (s + 1)] = piece
        tt[:, 512 * s : 512 * (s + 1)] = piece * lane_scale(512 * s, 512)

    def owners(b):
        slot = lax.broadcasted_iota(i32, (1, CAP), 1)
        key = jnp.where(slot < live_ref[0:1, b : b + 1], jnp.concatenate([rows_ref[2 * b], rows_ref[2 * b + 1]], axis=1), -1)

        def pick(i, c):
            r = pl.multiple_of(i * 512, 512)
            hit = key == lax.broadcasted_iota(i32, (512, CAP), 0) + r
            pt[pl.ds(r, 512), b * CAP : (b + 1) * CAP] = jnp.where(hit, 1.0, 0.0).astype(bf16)
            return c

        lax.fori_loop(0, ROWS // 512, pick, 0)

    fetch[3].wait()

    def build(i, c):
        build_counts(pl.multiple_of(i * 128, 128), nbt_ref, val, ct)
        return c

    lax.fori_loop(0, ROWS // 128, build, 0)
    halo(0).start()
    stl[...] = jnp.dot(tt[...], ct[0:ROWS, :], preferred_element_type=f32)

    for i in (4, 5, 6):
        fetch[i].wait()
    wcat[0:D, :] = ws_ref[...]
    wcat[D : 2 * D, :] = wn_ref[...]
    wt[:, 0:D] = wn_ref[...].T
    wt[:, D : 2 * D] = ws_ref[...].T

    for b in (4, 1, 0, 2, 3):
        halo(b).wait()
        row = ROWS + b * CAP
        part_t = hr[b].T * lane_scale(row, CAP)
        more = jnp.dot(part_t, ct[row : row + CAP, :], preferred_element_type=f32)
        if b != 3:
            stl[...] += more
        else:
            xt[D : 2 * D, :] = ((stl[...] + more) * (1.0 / FAN)).astype(bf16)
    NB = 512

    def pre_of(i):
        l = i * NB
        both_in = jnp.concatenate([fv[l : l + NB, :], xt[D : 2 * D, l : l + NB].T], axis=1)
        return jnp.dot(both_in, wcat[...], preferred_element_type=f32)

    pre = pre_of(0)
    for i in range(ROWS // NB):
        l = i * NB
        later = pre_of(i + 1) if i + 1 < ROWS // NB else None
        sig = 0.5 + 0.5 * jnp.tanh(0.5 * pre)
        silu = pre * sig
        hidv[l : l + NB, :] = silu.astype(bf16)
        slope = sig + silu * (1.0 - sig)
        grad = (cotv[l : l + NB, :].astype(f32) * slope).astype(bf16)
        both = jnp.dot(grad, wt[...], preferred_element_type=f32)
        gm[l : l + NB, :] = (both[:, 0:D] * (1.0 / FAN)).astype(bf16)
        own[l : l + NB, :] = both[:, D : 2 * D]
        pre = later
        add = jnp.dot(xt[:, l : l + NB], grad, preferred_element_type=f32)
        gw[...] = add if i == 0 else gw[...] + add

    for c in range(GROUP):
        gwc[c] = gw[16 * c : 16 * c + 16, :].astype(bf16)

    def rs(j):
        return pltpu.make_async_remote_copy(
            src_ref=gwc.at[place(PLANE[j])], dst_ref=rsr.at[j], send_sem=rs_s.at[j], recv_sem=rs_r.at[j],
            device_id=(at_plane(PLANE[j]),), device_id_type=MESH)

    for j in range(GROUP - 1):
        rs(j).start()

    def spread(row, count):
        return jnp.dot(ct[row : row + count, :], gm[...], preferred_element_type=f32)

    def back(b):
        return pltpu.make_async_remote_copy(
            src_ref=bs.at[b], dst_ref=br.at[pl.ds(b * CAP, CAP)], send_sem=bs_s.at[b], recv_sem=bs_r.at[b],
            device_id=(partner_of(me, b),), device_id_type=MESH)

    for b in ORDER:
        row = ROWS + b * CAP
        g = spread(row, CAP)
        for lo, hi, factor in spans(row, row + CAP):
            bs[b, lo:hi] = (g[lo:hi] * factor).astype(bf16)
        if b:
            back(b).start()

    def local_back(s):
        g = spread(512 * s, 512)
        for lo, hi, factor in spans(512 * s, 512 * (s + 1)):
            own[512 * s + lo : 512 * s + hi, :] += g[lo:hi] * factor

    local_back(0)
    for b in (0, 1, 2):
        owners(b)
    for j in range(GROUP - 1):
        rs(j).wait()
    back(0).start()
    part = gwc[spot].astype(f32)
    for j in range(GROUP - 1):
        part = part + rsr[j].astype(f32)
    zr[z] = part.astype(bf16)

    def zx(j):
        return pltpu.make_async_remote_copy(
            src_ref=zr.at[z], dst_ref=zr.at[z], send_sem=z_s.at[j], recv_sem=z_r.at[j],
            device_id=(at_line(LINE[j]),), device_id_type=MESH)

    for j in range(ZS - 1):
        zx(j).start()
    for s in (1, 2, 3):
        local_back(s)
    for b in (3, 4):
        owners(b)

    def z_wait(j):
        zx(j).wait_send()
        pltpu.make_async_remote_copy(
            src_ref=zr.at[z], dst_ref=zr.at[line(LINE[j], True)], send_sem=z_s.at[j], recv_sem=z_r.at[j],
            device_id=(at_line(LINE[j], True),), device_id_type=MESH).wait_recv()

    for j in range(ZS - 1):
        z_wait(j)
    full = zr[0].astype(f32)
    for j in range(1, ZS):
        full = full + zr[j].astype(f32)
    pair[0] = full
    swap = pltpu.make_async_remote_copy(
        src_ref=pair.at[0], dst_ref=pair.at[1], send_sem=pair_sem.at[0], recv_sem=pair_sem.at[1],
        device_id=(twin,), device_id_type=MESH)
    swap.start()
    swap.wait()
    agr[spot] = ((pair[0] + pair[1]) * (2.0**-9.5)).astype(bf16)

    def ag(j):
        return pltpu.make_async_remote_copy(
            src_ref=agr.at[spot], dst_ref=agr.at[spot], send_sem=ag_s.at[j], recv_sem=ag_r.at[j],
            device_id=(at_plane(PLANE[j]),), device_id_type=MESH)

    for j in range(GROUP - 1):
        ag(j).start()

    for b in ORDER:
        back(b).wait()

    for i in range(ROWS // NB):
        own[NB * i : NB * (i + 1), :] += jnp.dot(
            pt[NB * i : NB * (i + 1), :], br[...], preferred_element_type=f32)

    def ag_wait(j):
        ag(j).wait_send()
        pltpu.make_async_remote_copy(
            src_ref=agr.at[spot], dst_ref=agr.at[place(PLANE[j], True)], send_sem=ag_s.at[j], recv_sem=ag_r.at[j],
            device_id=(at_plane(PLANE[j], True),), device_id_type=MESH).wait_recv()

    for j in range(GROUP - 1):
        ag_wait(j)
    for c in range(GROUP):
        ref = gws_ref if c < GROUP // 2 else gwn_ref
        r = 16 * (c % (GROUP // 2))
        ref[r : r + 16, :] = agr[c].astype(f32)


def hand_over(hid, gf, gws, gwn, hid_out, gf_out, gws_out, gwn_out, sem):
    copies = [
        pltpu.make_async_copy(src, dst, sem.at[i])
        for i, (src, dst) in enumerate(((hid, hid_out), (gf, gf_out), (gws, gws_out), (gwn, gwn_out)))
    ]
    for one in copies:
        one.start()
    for one in copies:
        one.wait()


def on_device(features, w_self, w_neigh, cotangent, neighbours, send_rows, send_count):
    vmem = pl.BlockSpec(memory_space=pltpu.VMEM)
    hbm = pl.BlockSpec(memory_space=pl.ANY)
    dma = pltpu.SemaphoreType.DMA
    shapes = (((ROWS, H), bf16), ((ROWS, D), f32), ((D, H), f32), ((D, H), f32))
    call = pl.pallas_call(
        kernel,
        out_shape=tuple(pltpu.VMEM(*one) for one in shapes),
        in_specs=[hbm] * 7,
        out_specs=(vmem,) * 4,
        scratch_shapes=[
            pltpu.VMEM((D, H), bf16),
            pltpu.VMEM((D, H), bf16),
            pltpu.VMEM((FAN, ROWS), i32),
            pltpu.VMEM((2 * ROUNDS, 1, CAP // 2), i32),
            pltpu.VMEM((1, ROUNDS), i32),
            pltpu.VMEM((D, ROWS), f32),
            pltpu.VMEM((EXT, ROWS), bf16),
            pltpu.VMEM((ROWS, ROUNDS * CAP), bf16),
            pltpu.VMEM((ROWS, D), bf16),
            pltpu.VMEM((2 * D, ROWS), bf16),
            pltpu.VMEM((D, ROWS), bf16),
            pltpu.VMEM((ROWS, H), bf16),
            pltpu.VMEM((ROWS, D), bf16),
            pltpu.VMEM((ROUNDS, CAP, D), bf16),
            pltpu.VMEM((ROUNDS, CAP, D), bf16),
            pltpu.VMEM((ROUNDS, CAP, D), bf16),
            pltpu.VMEM((ROUNDS * CAP, D), bf16),
            pltpu.VMEM((2 * D, H), bf16),
            pltpu.VMEM((H, 2 * D), bf16),
            pltpu.VMEM((1 + WORDS, FAN, 128), i32),
            pltpu.VMEM((2 * D, H), f32),
            pltpu.VMEM((GROUP, 16, H), bf16),
            pltpu.VMEM((GROUP, 16, H), bf16),
            pltpu.VMEM((ZS, 16, H), bf16),
            pltpu.VMEM((2, 16, H), f32),
            pltpu.VMEM((GROUP, 16, H), bf16),
            pltpu.SMEM((2 * ROUNDS, 1, CAP // 2), i32),
            pltpu.VMEM((ROWS, D), f32),
            pltpu.VMEM((CAP, D), f32),
            dma((8,)),
            dma((ROUNDS,)), dma((ROUNDS,)), dma((ROUNDS,)), dma((ROUNDS,)),
            dma((GROUP,)), dma((GROUP,)), dma((ZS,)), dma((ZS,)), dma((2,)), dma((GROUP,)), dma((GROUP,)),
        ],
        compiler_params=pltpu.CompilerParams(
            collective_id=0, has_side_effects=True, vmem_limit_bytes=48 * 1024 * 1024),
        cost_estimate=pl.CostEstimate(flops=4_500_000_000, bytes_accessed=6_000_000, transcendentals=1_000_000),
    )
    args = (features, w_self, w_neigh, cotangent, neighbours.T, send_rows.reshape(2 * ROUNDS, 1, CAP // 2), send_count)
    args = tuple(pltpu.with_memory_space_constraint(one, pltpu.HBM) for one in args)
    return pl.pallas_call(
        hand_over,
        out_shape=tuple(pltpu.HBM(*one) for one in shapes),
        in_specs=[vmem] * 4,
        out_specs=(hbm,) * 4,
        scratch_shapes=[dma((4,))],
    )(*[pltpu.with_memory_space_constraint(one, pltpu.VMEM) for one in call(*args)])


def solution(mesh):
    placed = (
        P("dom", None), P(), P(), P("dom", None), P("dom", None), P("dom", None, None), P("dom", None),
    )
    return jax.shard_map(
        on_device,
        mesh=mesh,
        in_specs=placed,
        out_specs=(P("dom", None), P("dom", None), P(), P()),
        check_vma=False,
    )
```

```python
import functools

import jax
import jax.numpy as jnp
from jax import lax
from jax.experimental import pallas as pl
from jax.experimental.pallas import tpu as pltpu
from jax.sharding import PartitionSpec as P

FAN = 10
ROUNDS = 5
CAP = 256
ROWS = 2048
EXT = ROWS + ROUNDS * CAP
D = 128
H = 256
GROUP = 16
ZS = 8
WORDS = 13
DIGITS = 8
SPAN = EXT // DIGITS
MESH = pl.DeviceIdType.MESH
f32, bf16, i32 = jnp.float32, jnp.bfloat16, jnp.int32
ORDER = (3, 2, 1, 4, 0)


def ring(step, size):
    return min(step, size - step)


PLANE = sorted(
    ((dy, dx) for dy in range(4) for dx in range(4)),
    key=lambda t: (t != (0, 0), ring(t[0], 4) + ring(t[1], 4)), reverse=True)
LINE = sorted(range(8), key=lambda t: (t != 0, ring(t, 8)), reverse=True)


def partner_of(me, b):
    bit = lax.rem(lax.div(me, 2**b), 2)
    return me + (1 - 2 * bit) * 2**b


def power(digit):
    return min(digit, 6)


def spans(start, stop):
    cuts = [start] + [d * SPAN for d in range(1, DIGITS) if start < d * SPAN < stop] + [stop]
    return [(lo - start, hi - start, 16.0 ** -power(lo // SPAN)) for lo, hi in zip(cuts[:-1], cuts[1:])]


def lane_scale(start, count):
    row = lax.broadcasted_iota(i32, (1, count), 1)
    out = jnp.zeros((1, count), f32)
    for lo, hi, factor in spans(start, start + count):
        out = jnp.where(row >= lo, factor, out)
    return out.astype(bf16)


def build_counts(l, nbt_ref, val_ref, ct_ref):
    nb = nbt_ref[:, pl.ds(l, 128)]
    digit = (nb * 2521) >> 20
    rest = nb - digit * SPAN
    one = jnp.int32(1) << (4 * digit)
    group = rest >> 5
    val_ref[0] = rest & 31
    for q in range(WORDS):
        val_ref[1 + q] = jnp.where(group == q, one, 0)
    for half in range(2):
        rid = lax.broadcasted_iota(i32, (16, 128), 0) + 16 * half
        acc = [jnp.zeros((16, 128), i32)] * WORDS
        for k in range(FAN):
            hit = val_ref[0, k : k + 1, :] == rid
            for q in range(WORDS):
                acc[q] = acc[q] + jnp.where(hit, val_ref[1 + q, k : k + 1, :], 0)
        for q in range(WORDS):
            for s in range(DIGITS):
                row = s * SPAN + q * 32 + half * 16
                word = acc[q] if s < 7 else lax.shift_right_logical(acc[q], jnp.int32(4))
                count = word & jnp.int32(15 << (4 * power(s)))
                ct_ref[row : row + 16, pl.ds(l, 128)] = count.astype(f32).astype(bf16)


def kernel(
    feat_hbm, ws_hbm, wn_hbm, cot_hbm, nbt_hbm, rows_hbm, live_hbm,
    hidv, own, gws_ref, gwn_ref,
    ws_ref, wn_ref, nbt_ref, rows_ref, live_ref, stl, ct, pt, fv, xt, tt, cotv, gm, hs, hr, bs, br,
    wcat, wt, val, gw, gwc, rsr, zr, pair, agr, rows_s, ff, picked,
    in_sem, hs_s, hs_r, bs_s, bs_r, rs_s, rs_r, z_s, z_r, pair_sem, ag_s, ag_r,
):
    fetch = [
        pltpu.make_async_copy(src, dst, in_sem.at[i])
        for i, (src, dst) in enumerate((
            (rows_hbm, rows_ref), (live_hbm, live_ref), (feat_hbm, fv), (nbt_hbm, nbt_ref),
            (ws_hbm, ws_ref), (wn_hbm, wn_ref), (cot_hbm, cotv), (rows_hbm, rows_s)))
    ]
    for i in (2, 7, 0, 1, 3, 4, 5, 6):
        fetch[i].start()

    me = lax.axis_index("dom")
    core = lax.rem(me, 2)
    z = lax.rem(lax.div(me, 2), ZS)
    x = lax.rem(lax.div(me, 16), 4)
    y = lax.div(me, 64)
    zs = [z] + [lax.rem(z + d, ZS) for d in range(1, ZS)]
    xs = [x] + [lax.rem(x + d, 4) for d in range(1, 4)]
    ys = [y] + [lax.rem(y + d, 4) for d in range(1, 4)]
    spot = y * 4 + x
    twin = me + 1 - 2 * core

    def turned(step, back):
        return ((4 - step[0]) % 4, (4 - step[1]) % 4) if back else step

    def at_plane(step, back=False):
        dy, dx = turned(step, back)
        return ys[dy] * 64 + xs[dx] * 16 + z * 2 + core

    def place(step, back=False):
        dy, dx = turned(step, back)
        return ys[dy] * 4 + xs[dx]

    def line(step, back=False):
        return zs[(ZS - step) % ZS if back else step]

    def at_line(step, back=False):
        return y * 64 + x * 16 + line(step, back) * 2 + core

    barrier = pltpu.get_barrier_semaphore()
    for step in LINE[:-1]:
        pl.semaphore_signal(barrier, inc=1, device_id=(at_line(step),), device_id_type=MESH)
    for step in PLANE[:-1]:
        pl.semaphore_signal(barrier, inc=1, device_id=(at_plane(step),), device_id_type=MESH)

    pl.semaphore_signal(barrier, inc=1, device_id=(twin,), device_id_type=MESH)

    def halo(b):
        return pltpu.make_async_remote_copy(
            src_ref=hs.at[b], dst_ref=hr.at[b], send_sem=hs_s.at[b], recv_sem=hs_r.at[b],
            device_id=(partner_of(me, b),), device_id_type=MESH)

    fetch[2].wait()
    ff[...] = fv[...].astype(f32)
    for i in (0, 1, 7):
        fetch[i].wait()
    for b in ORDER:
        def load(i, c, b=b):
            r = pl.multiple_of(i * 128, 128)
            for t in range(128):
                picked[pl.ds(r + t, 1), :] = ff[pl.ds(rows_s[2 * b + i, 0, t], 1), :]
            return c

        lax.fori_loop(0, CAP // 128, load, 0)
        live = lax.broadcasted_iota(i32, (CAP, D), 0) < live_ref[0:1, b : b + 1]
        hs[b] = jnp.where(live, picked[...], 0.0).astype(bf16)

    for s in range(4):
        piece = fv[512 * s : 512 * (s + 1), :].T
        xt[0:D, 512 * s : 512 * (s + 1)] = piece
        tt[:, 512 * s : 512 * (s + 1)] = piece * lane_scale(512 * s, 512)

    def owners(b):
        slot = lax.broadcasted_iota(i32, (1, CAP), 1)
        key = jnp.where(slot < live_ref[0:1, b : b + 1], jnp.concatenate([rows_ref[2 * b], rows_ref[2 * b + 1]], axis=1), -1)

        def pick(i, c):
            r = pl.multiple_of(i * 512, 512)
            hit = key == lax.broadcasted_iota(i32, (512, CAP), 0) + r
            pt[pl.ds(r, 512), b * CAP : (b + 1) * CAP] = jnp.where(hit, 1.0, 0.0).astype(bf16)
            return c

        lax.fori_loop(0, ROWS // 512, pick, 0)

    for b in (0, 1):
        owners(b)
    pl.semaphore_wait(barrier, GROUP + ZS - 1)
    for b in ORDER[:-1]:
        halo(b).start()
    fetch[3].wait()

    def build(i, c):
        build_counts(pl.multiple_of(i * 128, 128), nbt_ref, val, ct)
        return c

    lax.fori_loop(0, ROWS // 128, build, 0)
    halo(0).start()
    stl[...] = jnp.dot(tt[...], ct[0:ROWS, :], preferred_element_type=f32)

    for i in (4, 5, 6):
        fetch[i].wait()
    wcat[0:D, :] = ws_ref[...]
    wcat[D : 2 * D, :] = wn_ref[...]
    wt[:, 0:D] = wn_ref[...].T
    wt[:, D : 2 * D] = ws_ref[...].T

    for b in (4, 1, 0, 2, 3):
        halo(b).wait()
        row = ROWS + b * CAP
        part_t = hr[b].T * lane_scale(row, CAP)
        more = jnp.dot(part_t, ct[row : row + CAP, :], preferred_element_type=f32)
        if b != 3:
            stl[...] += more
        else:
            xt[D : 2 * D, :] = ((stl[...] + more) * (1.0 / FAN)).astype(bf16)
    NB = 512

    def pre_of(i):
        l = i * NB
        both_in = jnp.concatenate([fv[l : l + NB, :], xt[D : 2 * D, l : l + NB].T], axis=1)
        return jnp.dot(both_in, wcat[...], preferred_element_type=f32)

    pre = pre_of(0)
    for i in range(ROWS // NB):
        l = i * NB
        later = pre_of(i + 1) if i + 1 < ROWS // NB else None
        sig = 0.5 + 0.5 * jnp.tanh(0.5 * pre)
        silu = pre * sig
        hidv[l : l + NB, :] = silu.astype(bf16)
        slope = sig + silu * (1.0 - sig)
        grad = (cotv[l : l + NB, :].astype(f32) * slope).astype(bf16)
        both = jnp.dot(grad, wt[...], preferred_element_type=f32)
        gm[l : l + NB, :] = (both[:, 0:D] * (1.0 / FAN)).astype(bf16)
        own[l : l + NB, :] = both[:, D : 2 * D]
        pre = later
        add = jnp.dot(xt[:, l : l + NB], grad, preferred_element_type=f32)
        gw[...] = add if i == 0 else gw[...] + add

    for c in range(GROUP):
        gwc[c] = gw[16 * c : 16 * c + 16, :].astype(bf16)

    def rs(j):
        return pltpu.make_async_remote_copy(
            src_ref=gwc.at[place(PLANE[j])], dst_ref=rsr.at[j], send_sem=rs_s.at[j], recv_sem=rs_r.at[j],
            device_id=(at_plane(PLANE[j]),), device_id_type=MESH)

    for j in range(GROUP - 1):
        rs(j).start()

    def spread(row, count):
        return jnp.dot(ct[row : row + count, :], gm[...], preferred_element_type=f32)

    def back(b):
        return pltpu.make_async_remote_copy(
            src_ref=bs.at[b], dst_ref=br.at[pl.ds(b * CAP, CAP)], send_sem=bs_s.at[b], recv_sem=bs_r.at[b],
            device_id=(partner_of(me, b),), device_id_type=MESH)

    for b in ORDER:
        row = ROWS + b * CAP
        g = spread(row, CAP)
        for lo, hi, factor in spans(row, row + CAP):
            bs[b, lo:hi] = (g[lo:hi] * factor).astype(bf16)
        if b:
            back(b).start()

    def local_back(s):
        g = spread(512 * s, 512)
        for lo, hi, factor in spans(512 * s, 512 * (s + 1)):
            own[512 * s + lo : 512 * s + hi, :] += g[lo:hi] * factor

    local_back(0)
    for b in (2,):
        owners(b)
    for j in range(GROUP - 1):
        rs(j).wait()
    back(0).start()
    part = gwc[spot].astype(f32)
    for j in range(GROUP - 1):
        part = part + rsr[j].astype(f32)
    zr[z] = part.astype(bf16)

    def zx(j):
        return pltpu.make_async_remote_copy(
            src_ref=zr.at[z], dst_ref=zr.at[z], send_sem=z_s.at[j], recv_sem=z_r.at[j],
            device_id=(at_line(LINE[j]),), device_id_type=MESH)

    for j in range(ZS - 1):
        zx(j).start()
    for s in (1, 2, 3):
        local_back(s)
    for b in (3, 4):
        owners(b)

    def z_wait(j):
        zx(j).wait_send()
        pltpu.make_async_remote_copy(
            src_ref=zr.at[z], dst_ref=zr.at[line(LINE[j], True)], send_sem=z_s.at[j], recv_sem=z_r.at[j],
            device_id=(at_line(LINE[j], True),), device_id_type=MESH).wait_recv()

    for j in range(ZS - 1):
        z_wait(j)
    full = zr[0].astype(f32)
    for j in range(1, ZS):
        full = full + zr[j].astype(f32)
    pair[0] = full
    swap = pltpu.make_async_remote_copy(
        src_ref=pair.at[0], dst_ref=pair.at[1], send_sem=pair_sem.at[0], recv_sem=pair_sem.at[1],
        device_id=(twin,), device_id_type=MESH)
    swap.start()
    swap.wait()
    agr[spot] = ((pair[0] + pair[1]) * (2.0**-9.5)).astype(bf16)

    def ag(j):
        return pltpu.make_async_remote_copy(
            src_ref=agr.at[spot], dst_ref=agr.at[spot], send_sem=ag_s.at[j], recv_sem=ag_r.at[j],
            device_id=(at_plane(PLANE[j]),), device_id_type=MESH)

    for j in range(GROUP - 1):
        ag(j).start()

    for b in ORDER:
        back(b).wait()

    for i in range(ROWS // NB):
        own[NB * i : NB * (i + 1), :] += jnp.dot(
            pt[NB * i : NB * (i + 1), :], br[...], preferred_element_type=f32)

    def ag_wait(j):
        ag(j).wait_send()
        pltpu.make_async_remote_copy(
            src_ref=agr.at[spot], dst_ref=agr.at[place(PLANE[j], True)], send_sem=ag_s.at[j], recv_sem=ag_r.at[j],
            device_id=(at_plane(PLANE[j], True),), device_id_type=MESH).wait_recv()

    for j in range(GROUP - 1):
        ag_wait(j)
    for c in range(GROUP):
        ref = gws_ref if c < GROUP // 2 else gwn_ref
        r = 16 * (c % (GROUP // 2))
        ref[r : r + 16, :] = agr[c].astype(f32)


def hand_over(hid, gf, gws, gwn, hid_out, gf_out, gws_out, gwn_out, sem):
    copies = [
        pltpu.make_async_copy(src, dst, sem.at[i])
        for i, (src, dst) in enumerate(((hid, hid_out), (gf, gf_out), (gws, gws_out), (gwn, gwn_out)))
    ]
    for one in copies:
        one.start()
    for one in copies:
        one.wait()


def on_device(features, w_self, w_neigh, cotangent, neighbours, send_rows, send_count):
    vmem = pl.BlockSpec(memory_space=pltpu.VMEM)
    hbm = pl.BlockSpec(memory_space=pl.ANY)
    dma = pltpu.SemaphoreType.DMA
    shapes = (((ROWS, H), bf16), ((ROWS, D), f32), ((D, H), f32), ((D, H), f32))
    call = pl.pallas_call(
        kernel,
        out_shape=tuple(pltpu.VMEM(*one) for one in shapes),
        in_specs=[hbm] * 7,
        out_specs=(vmem,) * 4,
        scratch_shapes=[
            pltpu.VMEM((D, H), bf16),
            pltpu.VMEM((D, H), bf16),
            pltpu.VMEM((FAN, ROWS), i32),
            pltpu.VMEM((2 * ROUNDS, 1, CAP // 2), i32),
            pltpu.VMEM((1, ROUNDS), i32),
            pltpu.VMEM((D, ROWS), f32),
            pltpu.VMEM((EXT, ROWS), bf16),
            pltpu.VMEM((ROWS, ROUNDS * CAP), bf16),
            pltpu.VMEM((ROWS, D), bf16),
            pltpu.VMEM((2 * D, ROWS), bf16),
            pltpu.VMEM((D, ROWS), bf16),
            pltpu.VMEM((ROWS, H), bf16),
            pltpu.VMEM((ROWS, D), bf16),
            pltpu.VMEM((ROUNDS, CAP, D), bf16),
            pltpu.VMEM((ROUNDS, CAP, D), bf16),
            pltpu.VMEM((ROUNDS, CAP, D), bf16),
            pltpu.VMEM((ROUNDS * CAP, D), bf16),
            pltpu.VMEM((2 * D, H), bf16),
            pltpu.VMEM((H, 2 * D), bf16),
            pltpu.VMEM((1 + WORDS, FAN, 128), i32),
            pltpu.VMEM((2 * D, H), f32),
            pltpu.VMEM((GROUP, 16, H), bf16),
            pltpu.VMEM((GROUP, 16, H), bf16),
            pltpu.VMEM((ZS, 16, H), bf16),
            pltpu.VMEM((2, 16, H), f32),
            pltpu.VMEM((GROUP, 16, H), bf16),
            pltpu.SMEM((2 * ROUNDS, 1, CAP // 2), i32),
            pltpu.VMEM((ROWS, D), f32),
            pltpu.VMEM((CAP, D), f32),
            dma((8,)),
            dma((ROUNDS,)), dma((ROUNDS,)), dma((ROUNDS,)), dma((ROUNDS,)),
            dma((GROUP,)), dma((GROUP,)), dma((ZS,)), dma((ZS,)), dma((2,)), dma((GROUP,)), dma((GROUP,)),
        ],
        compiler_params=pltpu.CompilerParams(
            collective_id=0, has_side_effects=True, vmem_limit_bytes=48 * 1024 * 1024),
        cost_estimate=pl.CostEstimate(flops=4_500_000_000, bytes_accessed=6_000_000, transcendentals=1_000_000),
    )
    args = (features, w_self, w_neigh, cotangent, neighbours.T, send_rows.reshape(2 * ROUNDS, 1, CAP // 2), send_count)
    args = tuple(pltpu.with_memory_space_constraint(one, pltpu.HBM) for one in args)
    return pl.pallas_call(
        hand_over,
        out_shape=tuple(pltpu.HBM(*one) for one in shapes),
        in_specs=[vmem] * 4,
        out_specs=(hbm,) * 4,
        scratch_shapes=[dma((4,))],
    )(*[pltpu.with_memory_space_constraint(one, pltpu.VMEM) for one in call(*args)])


def solution(mesh):
    placed = (
        P("dom", None), P(), P(), P("dom", None), P("dom", None), P("dom", None, None), P("dom", None),
    )
    return jax.shard_map(
        on_device,
        mesh=mesh,
        in_specs=placed,
        out_specs=(P("dom", None), P("dom", None), P(), P()),
        check_vma=False,
    )
```

```python
import functools

import jax
import jax.numpy as jnp
from jax import lax
from jax.experimental import pallas as pl
from jax.experimental.pallas import tpu as pltpu
from jax.sharding import PartitionSpec as P

FAN = 10
ROUNDS = 5
CAP = 256
ROWS = 2048
EXT = ROWS + ROUNDS * CAP
D = 128
H = 256
GROUP = 16
ZS = 8
WORDS = 13
DIGITS = 8
SPAN = EXT // DIGITS
MESH = pl.DeviceIdType.MESH
f32, bf16, i32 = jnp.float32, jnp.bfloat16, jnp.int32
ORDER = (3, 2, 1, 4, 0)


def ring(step, size):
    return min(step, size - step)


PLANE = sorted(
    ((dy, dx) for dy in range(4) for dx in range(4)),
    key=lambda t: (t != (0, 0), ring(t[0], 4) + ring(t[1], 4)), reverse=True)
LINE = sorted(range(8), key=lambda t: (t != 0, ring(t, 8)), reverse=True)


def partner_of(me, b):
    bit = lax.rem(lax.div(me, 2**b), 2)
    return me + (1 - 2 * bit) * 2**b


def power(digit):
    return min(digit, 6)


def spans(start, stop):
    cuts = [start] + [d * SPAN for d in range(1, DIGITS) if start < d * SPAN < stop] + [stop]
    return [(lo - start, hi - start, 16.0 ** -power(lo // SPAN)) for lo, hi in zip(cuts[:-1], cuts[1:])]


def lane_scale(start, count):
    row = lax.broadcasted_iota(i32, (1, count), 1)
    out = jnp.zeros((1, count), f32)
    for lo, hi, factor in spans(start, start + count):
        out = jnp.where(row >= lo, factor, out)
    return out.astype(bf16)


def build_counts(l, nbt_ref, val_ref, ct_ref):
    nb = nbt_ref[:, pl.ds(l, 128)]
    digit = (nb * 2521) >> 20
    rest = nb - digit * SPAN
    one = jnp.int32(1) << (4 * digit)
    group = rest >> 5
    val_ref[0] = rest & 31
    for q in range(WORDS):
        val_ref[1 + q] = jnp.where(group == q, one, 0)
    for half in range(2):
        rid = lax.broadcasted_iota(i32, (16, 128), 0) + 16 * half
        acc = [jnp.zeros((16, 128), i32)] * WORDS
        for k in range(FAN):
            hit = val_ref[0, k : k + 1, :] == rid
            for q in range(WORDS):
                acc[q] = acc[q] + jnp.where(hit, val_ref[1 + q, k : k + 1, :], 0)
        for q in range(WORDS):
            for s in range(DIGITS):
                row = s * SPAN + q * 32 + half * 16
                word = acc[q] if s < 7 else lax.shift_right_logical(acc[q], jnp.int32(4))
                count = word & jnp.int32(15 << (4 * power(s)))
                ct_ref[row : row + 16, pl.ds(l, 128)] = count.astype(f32).astype(bf16)


def kernel(
    feat_hbm, ws_hbm, wn_hbm, cot_hbm, nbt_hbm, rows_hbm, live_hbm,
    hidv, own, gws_ref, gwn_ref,
    ws_ref, wn_ref, nbt_ref, rows_ref, live_ref, stl, ct, pt, fv, xt, tt, cotv, gm, hs, hr, bs, br,
    wcat, wt, val, gw, gwc, rsr, zr, pair, agr, rows_s, ff, picked,
    in_sem, hs_s, hs_r, bs_s, bs_r, rs_s, rs_r, z_s, z_r, pair_sem, ag_s, ag_r,
):
    fetch = [
        pltpu.make_async_copy(src, dst, in_sem.at[i])
        for i, (src, dst) in enumerate((
            (rows_hbm, rows_ref), (live_hbm, live_ref), (feat_hbm, fv), (nbt_hbm, nbt_ref),
            (ws_hbm, ws_ref), (wn_hbm, wn_ref), (cot_hbm, cotv), (rows_hbm, rows_s)))
    ]
    for i in (2, 7, 0, 1, 3, 4, 5, 6):
        fetch[i].start()

    me = lax.axis_index("dom")
    core = lax.rem(me, 2)
    z = lax.rem(lax.div(me, 2), ZS)
    x = lax.rem(lax.div(me, 16), 4)
    y = lax.div(me, 64)
    zs = [z] + [lax.rem(z + d, ZS) for d in range(1, ZS)]
    xs = [x] + [lax.rem(x + d, 4) for d in range(1, 4)]
    ys = [y] + [lax.rem(y + d, 4) for d in range(1, 4)]
    spot = y * 4 + x
    twin = me + 1 - 2 * core

    def turned(step, back):
        return ((4 - step[0]) % 4, (4 - step[1]) % 4) if back else step

    def at_plane(step, back=False):
        dy, dx = turned(step, back)
        return ys[dy] * 64 + xs[dx] * 16 + z * 2 + core

    def place(step, back=False):
        dy, dx = turned(step, back)
        return ys[dy] * 4 + xs[dx]

    def line(step, back=False):
        return zs[(ZS - step) % ZS if back else step]

    def at_line(step, back=False):
        return y * 64 + x * 16 + line(step, back) * 2 + core

    barrier = pltpu.get_barrier_semaphore()
    for step in LINE[:-1]:
        pl.semaphore_signal(barrier, inc=1, device_id=(at_line(step),), device_id_type=MESH)
    for step in PLANE[:-1]:
        pl.semaphore_signal(barrier, inc=1, device_id=(at_plane(step),), device_id_type=MESH)

    pl.semaphore_signal(barrier, inc=1, device_id=(twin,), device_id_type=MESH)

    def halo(b):
        return pltpu.make_async_remote_copy(
            src_ref=hs.at[b], dst_ref=hr.at[b], send_sem=hs_s.at[b], recv_sem=hs_r.at[b],
            device_id=(partner_of(me, b),), device_id_type=MESH)

    fetch[2].wait()
    ff[...] = fv[...].astype(f32)
    for i in (0, 1, 7):
        fetch[i].wait()
    for b in ORDER:
        def load(i, c, b=b):
            r = pl.multiple_of(i * 128, 128)
            for t in range(128):
                picked[pl.ds(r + t, 1), :] = ff[pl.ds(rows_s[2 * b + i, 0, t], 1), :]
            return c

        lax.fori_loop(0, CAP // 128, load, 0)
        live = lax.broadcasted_iota(i32, (CAP, D), 0) < live_ref[0:1, b : b + 1]
        hs[b] = jnp.where(live, picked[...], 0.0).astype(bf16)

    for s in range(4):
        piece = fv[512 * s : 512 * (s + 1), :].T
        xt[0:D, 512 * s : 512 * (s + 1)] = piece
        tt[:, 512 * s : 512 * (s + 1)] = piece * lane_scale(512 * s, 512)

    def owners(b):
        slot = lax.broadcasted_iota(i32, (1, CAP), 1)
        key = jnp.where(slot < live_ref[0:1, b : b + 1], jnp.concatenate([rows_ref[2 * b], rows_ref[2 * b + 1]], axis=1), -1)

        def pick(i, c):
            r = pl.multiple_of(i * 512, 512)
            hit = key == lax.broadcasted_iota(i32, (512, CAP), 0) + r
            pt[pl.ds(r, 512), b * CAP : (b + 1) * CAP] = jnp.where(hit, 1.0, 0.0).astype(bf16)
            return c

        lax.fori_loop(0, ROWS // 512, pick, 0)

    for b in (0, 1):
        owners(b)
    pl.semaphore_wait(barrier, GROUP + ZS - 1)
    for b in ORDER[:-1]:
        halo(b).start()
    fetch[3].wait()

    def build(i, c):
        build_counts(pl.multiple_of(i * 128, 128), nbt_ref, val, ct)
        return c

    lax.fori_loop(0, ROWS // 128, build, 0)
    halo(0).start()
    stl[...] = jnp.dot(tt[...], ct[0:ROWS, :], preferred_element_type=f32)

    for i in (4, 5, 6):
        fetch[i].wait()
    wcat[0:D, :] = ws_ref[...]
    wcat[D : 2 * D, :] = wn_ref[...]
    wt[:, 0:D] = wn_ref[...].T
    wt[:, D : 2 * D] = ws_ref[...].T

    for b in (4, 1, 0, 2, 3):
        halo(b).wait()
        row = ROWS + b * CAP
        part_t = hr[b].T * lane_scale(row, CAP)
        more = jnp.dot(part_t, ct[row : row + CAP, :], preferred_element_type=f32)
        if b != 3:
            stl[...] += more
        else:
            xt[D : 2 * D, :] = ((stl[...] + more) * (1.0 / FAN)).astype(bf16)
    NB = 512

    def pre_of(i):
        l = i * NB
        both_in = jnp.concatenate([fv[l : l + NB, :], xt[D : 2 * D, l : l + NB].T], axis=1)
        return jnp.dot(both_in, wcat[...], preferred_element_type=f32)

    pre = pre_of(0)
    for i in range(ROWS // NB):
        l = i * NB
        later = pre_of(i + 1) if i + 1 < ROWS // NB else None
        sig = 0.5 + 0.5 * jnp.tanh(0.5 * pre)
        silu = pre * sig
        hidv[l : l + NB, :] = silu.astype(bf16)
        slope = sig + silu * (1.0 - sig)
        grad = (cotv[l : l + NB, :].astype(f32) * slope).astype(bf16)
        both = jnp.dot(grad, wt[...], preferred_element_type=f32)
        gm[l : l + NB, :] = (both[:, 0:D] * (1.0 / FAN)).astype(bf16)
        own[l : l + NB, :] = both[:, D : 2 * D]
        pre = later
        add = jnp.dot(xt[:, l : l + NB], grad, preferred_element_type=f32)
        gw[...] = add if i == 0 else gw[...] + add

    for c in range(GROUP):
        gwc[c] = gw[16 * c : 16 * c + 16, :].astype(bf16)

    def rs(j):
        return pltpu.make_async_remote_copy(
            src_ref=gwc.at[place(PLANE[j])], dst_ref=rsr.at[j], send_sem=rs_s.at[j], recv_sem=rs_r.at[j],
            device_id=(at_plane(PLANE[j]),), device_id_type=MESH)

    for j in range(GROUP - 1):
        rs(j).start()

    def spread(row, count):
        return jnp.dot(ct[row : row + count, :], gm[...], preferred_element_type=f32)

    def back(b):
        return pltpu.make_async_remote_copy(
            src_ref=bs.at[b], dst_ref=br.at[pl.ds(b * CAP, CAP)], send_sem=bs_s.at[b], recv_sem=bs_r.at[b],
            device_id=(partner_of(me, b),), device_id_type=MESH)

    for b in ORDER:
        row = ROWS + b * CAP
        g = spread(row, CAP)
        for lo, hi, factor in spans(row, row + CAP):
            bs[b, lo:hi] = (g[lo:hi] * factor).astype(bf16)
        if b:
            back(b).start()

    def local_back(s):
        g = spread(512 * s, 512)
        for lo, hi, factor in spans(512 * s, 512 * (s + 1)):
            own[512 * s + lo : 512 * s + hi, :] += g[lo:hi] * factor

    local_back(0)
    for b in (2,):
        owners(b)
    for j in range(GROUP - 1):
        rs(j).wait()
    back(0).start()
    part = gwc[spot].astype(f32)
    for j in range(GROUP - 1):
        part = part + rsr[j].astype(f32)
    zr[z] = part.astype(bf16)

    def zx(j):
        return pltpu.make_async_remote_copy(
            src_ref=zr.at[z], dst_ref=zr.at[z], send_sem=z_s.at[j], recv_sem=z_r.at[j],
            device_id=(at_line(LINE[j]),), device_id_type=MESH)

    for j in range(ZS - 1):
        zx(j).start()
    for s in (1, 2):
        local_back(s)
    for b in (3, 4):
        owners(b)

    def z_wait(j):
        zx(j).wait_send()
        pltpu.make_async_remote_copy(
            src_ref=zr.at[z], dst_ref=zr.at[line(LINE[j], True)], send_sem=z_s.at[j], recv_sem=z_r.at[j],
            device_id=(at_line(LINE[j], True),), device_id_type=MESH).wait_recv()

    for j in range(ZS - 1):
        z_wait(j)
    full = zr[0].astype(f32)
    for j in range(1, ZS):
        full = full + zr[j].astype(f32)
    pair[0] = full
    swap = pltpu.make_async_remote_copy(
        src_ref=pair.at[0], dst_ref=pair.at[1], send_sem=pair_sem.at[0], recv_sem=pair_sem.at[1],
        device_id=(twin,), device_id_type=MESH)
    swap.start()
    local_back(3)
    swap.wait()
    agr[spot] = ((pair[0] + pair[1]) * (2.0**-9.5)).astype(bf16)

    def ag(j):
        return pltpu.make_async_remote_copy(
            src_ref=agr.at[spot], dst_ref=agr.at[spot], send_sem=ag_s.at[j], recv_sem=ag_r.at[j],
            device_id=(at_plane(PLANE[j]),), device_id_type=MESH)

    for j in range(GROUP - 1):
        ag(j).start()

    for b in ORDER:
        back(b).wait()

    for i in range(ROWS // NB):
        own[NB * i : NB * (i + 1), :] += jnp.dot(
            pt[NB * i : NB * (i + 1), :], br[...], preferred_element_type=f32)

    def ag_wait(j):
        ag(j).wait_send()
        pltpu.make_async_remote_copy(
            src_ref=agr.at[spot], dst_ref=agr.at[place(PLANE[j], True)], send_sem=ag_s.at[j], recv_sem=ag_r.at[j],
            device_id=(at_plane(PLANE[j], True),), device_id_type=MESH).wait_recv()

    for j in range(GROUP - 1):
        ag_wait(j)
    for c in range(GROUP):
        ref = gws_ref if c < GROUP // 2 else gwn_ref
        r = 16 * (c % (GROUP // 2))
        ref[r : r + 16, :] = agr[c].astype(f32)


def hand_over(hid, gf, gws, gwn, hid_out, gf_out, gws_out, gwn_out, sem):
    copies = [
        pltpu.make_async_copy(src, dst, sem.at[i])
        for i, (src, dst) in enumerate(((hid, hid_out), (gf, gf_out), (gws, gws_out), (gwn, gwn_out)))
    ]
    for one in copies:
        one.start()
    for one in copies:
        one.wait()


def on_device(features, w_self, w_neigh, cotangent, neighbours, send_rows, send_count):
    vmem = pl.BlockSpec(memory_space=pltpu.VMEM)
    hbm = pl.BlockSpec(memory_space=pl.ANY)
    dma = pltpu.SemaphoreType.DMA
    shapes = (((ROWS, H), bf16), ((ROWS, D), f32), ((D, H), f32), ((D, H), f32))
    call = pl.pallas_call(
        kernel,
        out_shape=tuple(pltpu.VMEM(*one) for one in shapes),
        in_specs=[hbm] * 7,
        out_specs=(vmem,) * 4,
        scratch_shapes=[
            pltpu.VMEM((D, H), bf16),
            pltpu.VMEM((D, H), bf16),
            pltpu.VMEM((FAN, ROWS), i32),
            pltpu.VMEM((2 * ROUNDS, 1, CAP // 2), i32),
            pltpu.VMEM((1, ROUNDS), i32),
            pltpu.VMEM((D, ROWS), f32),
            pltpu.VMEM((EXT, ROWS), bf16),
            pltpu.VMEM((ROWS, ROUNDS * CAP), bf16),
            pltpu.VMEM((ROWS, D), bf16),
            pltpu.VMEM((2 * D, ROWS), bf16),
            pltpu.VMEM((D, ROWS), bf16),
            pltpu.VMEM((ROWS, H), bf16),
            pltpu.VMEM((ROWS, D), bf16),
            pltpu.VMEM((ROUNDS, CAP, D), bf16),
            pltpu.VMEM((ROUNDS, CAP, D), bf16),
            pltpu.VMEM((ROUNDS, CAP, D), bf16),
            pltpu.VMEM((ROUNDS * CAP, D), bf16),
            pltpu.VMEM((2 * D, H), bf16),
            pltpu.VMEM((H, 2 * D), bf16),
            pltpu.VMEM((1 + WORDS, FAN, 128), i32),
            pltpu.VMEM((2 * D, H), f32),
            pltpu.VMEM((GROUP, 16, H), bf16),
            pltpu.VMEM((GROUP, 16, H), bf16),
            pltpu.VMEM((ZS, 16, H), bf16),
            pltpu.VMEM((2, 16, H), f32),
            pltpu.VMEM((GROUP, 16, H), bf16),
            pltpu.SMEM((2 * ROUNDS, 1, CAP // 2), i32),
            pltpu.VMEM((ROWS, D), f32),
            pltpu.VMEM((CAP, D), f32),
            dma((8,)),
            dma((ROUNDS,)), dma((ROUNDS,)), dma((ROUNDS,)), dma((ROUNDS,)),
            dma((GROUP,)), dma((GROUP,)), dma((ZS,)), dma((ZS,)), dma((2,)), dma((GROUP,)), dma((GROUP,)),
        ],
        compiler_params=pltpu.CompilerParams(
            collective_id=0, has_side_effects=True, vmem_limit_bytes=48 * 1024 * 1024),
        cost_estimate=pl.CostEstimate(flops=4_500_000_000, bytes_accessed=6_000_000, transcendentals=1_000_000),
    )
    args = (features, w_self, w_neigh, cotangent, neighbours.T, send_rows.reshape(2 * ROUNDS, 1, CAP // 2), send_count)
    args = tuple(pltpu.with_memory_space_constraint(one, pltpu.HBM) for one in args)
    return pl.pallas_call(
        hand_over,
        out_shape=tuple(pltpu.HBM(*one) for one in shapes),
        in_specs=[vmem] * 4,
        out_specs=(hbm,) * 4,
        scratch_shapes=[dma((4,))],
    )(*[pltpu.with_memory_space_constraint(one, pltpu.VMEM) for one in call(*args)])


def solution(mesh):
    placed = (
        P("dom", None), P(), P(), P("dom", None), P("dom", None), P("dom", None, None), P("dom", None),
    )
    return jax.shard_map(
        on_device,
        mesh=mesh,
        in_specs=placed,
        out_specs=(P("dom", None), P("dom", None), P(), P()),
        check_vma=False,
    )
```
